32 devices in a mesh: dp: 16 (over z, y, x), tensor: 2 (over core).
Axes of the slice: x: 2, y: 2, z: 4, core: 2. Of those that a mesh axis runs over, the one named last changes fastest.
Arguments:
- layer_in: bfloat16 [16384, 768], P(('dp', 'tensor')), may hold values from -6 to 6
- seq_lens: int32 [16], P('dp'), may hold values from 256 to 1024, as said below
- w_qkv: bfloat16 [768, 3, 768], P('dp', None, 'tensor'), may hold values from -0.21875 to 0.21875
- b_qv: float32 [2, 768], replicated, may hold values from -1.5 to 1.5
- w_out: bfloat16 [768, 768], P('dp', 'tensor'), may hold values from -3.5 to 3.5
- b_out: float32 [768], replicated, may hold values from -2.5 to 2.5
- gain_one: float32 [768], replicated, may hold values from 0.25 to 1.75
- shift_one: float32 [768], replicated, may hold values from -1.5 to 1.5
- w_up: bfloat16 [768, 3072], P('dp', 'tensor'), may hold values from -0.21875 to 0.21875
- b_up: float32 [3072], replicated, may hold values from -2.5 to 2.5
- w_down: bfloat16 [768, 3072], P('dp', 'tensor'), may hold values from -0.109375 to 0.109375
- b_down: float32 [768], replicated, may hold values from -2.5 to 2.5
- gain_two: float32 [768], replicated, may hold values from 0.25 to 1.75
- shift_two: float32 [768], replicated, may hold values from -1.5 to 1.5
- cotangent: bfloat16 [16384, 768], P(('dp', 'tensor')), may hold values from -6 to 6
Outputs:
- output: bfloat16 [16384, 768], P(('dp', 'tensor'))
- grad_input: bfloat16 [16384, 768], P(('dp', 'tensor'))
- grad_w_qkv: float32 [768, 3, 768], P('dp', None, 'tensor')
- grad_b_qv: float32 [2, 768], P(None, 'tensor')
- grad_w_out: float32 [768, 768], P('dp', 'tensor')
- grad_b_out: float32 [768], replicated
- grad_gain_one: float32 [768], replicated
- grad_shift_one: float32 [768], replicated
- grad_w_up: float32 [768, 3072], P('dp', 'tensor')
- grad_b_up: float32 [3072], P('tensor')
- grad_w_down: float32 [768, 3072], P('dp', 'tensor')
- grad_b_down: float32 [768], replicated
- grad_gain_two: float32 [768], replicated
- grad_shift_two: float32 [768], replicated
The draws below stay inside these ranges and needn't reach their ends.
Inputs may be any that keep to these rules, and one draw needn't show every extreme that they name: Sequence g fills its first seq_lens[g] slots, the rest is padding; some sequence has all 1024 slots and some has 256.
All inputs are finite; a program needn't handle non-finite values.
Results may differ from the reference program's by a relative error of at most 0.019.
Values may be sent and summed in bfloat16 or wider, within the bound.
No kernel may reach another device: no remote copies, remote signals or barrier semaphores. Data moves between devices by JAX's collectives and lax.ppermute only.
A program may use at most 128 MiB of HBM per device.

```python
import jax
import jax.numpy as jnp
from jax import lax

D = 768
HEADS = 12
HEAD_DIM = 64
FF = 3072
SEQ = 1024
TOKENS = 16384
N_DP = 16


def draw_seq_lens(key, part):
    key = jax.random.fold_in(key, 7)
    first, second, third = jax.random.split(key, 3)
    lengths = jax.random.randint(first, (N_DP,), SEQ // 4, SEQ + 1)
    longest = jax.random.randint(second, (), 0, N_DP)
    offset = jax.random.randint(third, (), 1, N_DP)
    shortest = (longest + offset) % N_DP
    lengths = lengths.at[longest].set(SEQ).at[shortest].set(SEQ // 4)
    return lengths.astype(jnp.int32)


def raised(array, own_key, source, target, shards_of, factor):
    def block_of(axis_at):
        return (jnp.arange(array.shape[axis_at]) // (array.shape[axis_at] // shards_of)).reshape((-1,) + (1,) * (array.ndim - 1 - axis_at))

    first = jax.random.permutation(own_key, shards_of)[block_of(target)]
    other_side = (block_of(target) + shards_of // 2) % shards_of
    return jnp.where((block_of(source) == first) | (block_of(source) == other_side), factor * array, array)


def level_of(own_key, shape, cuts, least, largest):
    level = 1.0
    for dim, shards_of in cuts:
        steps = jax.random.uniform(jax.random.fold_in(jax.random.fold_in(own_key, 6), dim), (shards_of,), jnp.float32, least / len(cuts), largest / len(cuts))
        level = level * jnp.repeat(jnp.exp(steps), shape[dim] // shards_of).reshape((-1,) + (1,) * (len(shape) - 1 - dim))
    return level


def normal_values(stream_key, dims, scale, limit, cuts=(), kind=jnp.bfloat16):
    level = level_of(stream_key, dims, cuts, -0.22, 0.18) if cuts else 1.0
    result = jax.random.normal(stream_key, dims, jnp.float32) * scale * level
    return jnp.minimum(jnp.maximum(result, -limit), limit).astype(kind)


def bell_draw_with(rng, shape, scale, bound, cuts, heavy, kind=jnp.bfloat16):
    array = scale * jax.random.normal(rng, shape, jnp.float32)
    if cuts:
        array = array * level_of(rng, shape, cuts, -0.22, 0.18)
    return jnp.clip(raised(array, jax.random.fold_in(rng, 3), *heavy), -bound, bound).astype(kind)


def setup_inputs(seed: int = 0) -> dict:
    splits = jax.random.split(jax.random.key(seed), 16)
    return {
        "layer_in": normal_values(splits[0], (TOKENS, D), 1.0, 6.0, ((0, 32),)),
        "seq_lens": draw_seq_lens(jax.random.fold_in(splits[15], 71), 0),
        "w_qkv": normal_values(splits[2], (D, 3, D), D ** -0.5, 0.21875, ((0, 16), (2, 2))),
        "b_qv": normal_values(splits[3], (2, D), 0.3, 1.5, (), jnp.float32),
        "w_out": normal_values(splits[4], (D, D), (max(D // 256, 1)) ** -0.5, 3.5, ((0, 16), (1, 2))),
        "b_out": normal_values(splits[5], (D,), 0.5, 2.5, (), jnp.float32),
        "gain_one": jnp.clip(1.0 + 0.15 * jax.random.normal(splits[6], (D,), jnp.float32), 0.25, 1.75),
        "shift_one": normal_values(splits[7], (D,), 0.3, 1.5, (), jnp.float32),
        "w_up": normal_values(splits[8], (D, FF), D ** -0.5, 0.21875, ((0, 16), (1, 2))),
        "b_up": normal_values(splits[9], (FF,), 0.5, 2.5, (), jnp.float32),
        "w_down": normal_values(splits[10], (D, FF), FF ** -0.5, 0.109375, ((0, 16), (1, 2))),
        "b_down": normal_values(splits[11], (D,), 0.5, 2.5, (), jnp.float32),
        "gain_two": jnp.clip(1.0 + 0.15 * jax.random.normal(splits[12], (D,), jnp.float32), 0.25, 1.75),
        "shift_two": normal_values(splits[13], (D,), 0.3, 1.5, (), jnp.float32),
        "cotangent": bell_draw_with(splits[14], (TOKENS, D), 1.0, 6.0, ((0, 32),), (0, 1, 32, 2.75)),
    }


@jax.custom_vjp
def low(v):
    return lax.optimization_barrier(v.astype(jnp.bfloat16)).astype(jnp.float32)

@jax.custom_vjp
def low_back(v):
    return v

def low_keep(v):
    return (low(v), None)

def low_pass(kept, grad):
    return (grad,)

def back_keep(v):
    return (v, None)

def back_low(kept, grad):
    return (low(grad),)
low.defvjp(low_keep, low_pass)
low_back.defvjp(back_keep, back_low)
EPS = 1e-05
NEG = -1e+30

def norm_rows(v, gain, shift):
    mean = lax.optimization_barrier(jnp.mean(v, axis=-1, keepdims=True))
    centred = v - mean
    spread = lax.optimization_barrier(jnp.mean(centred * centred, axis=-1, keepdims=True))
    return centred * lax.rsqrt(spread + EPS) * gain + shift

def attend_group(pieces):
    query, keyed, valued, length = pieces
    scale = HEAD_DIM ** (-0.5)
    q_heads = query.reshape(SEQ, HEADS, HEAD_DIM)
    k_heads = keyed.reshape(SEQ, HEADS, HEAD_DIM)
    v_heads = valued.reshape(SEQ, HEADS, HEAD_DIM)
    scores = jnp.einsum('qhd,khd->hqk', q_heads, k_heads, precision=lax.Precision.HIGHEST) * scale
    keep = (jnp.arange(SEQ, dtype=jnp.int32) < length)[None, None, :]
    scores = low_back(jnp.where(keep, scores, NEG))
    top = lax.optimization_barrier(jnp.max(scores, axis=-1, keepdims=True))
    expo = jnp.exp(scores - top)
    probs = low(expo / lax.optimization_barrier(jnp.sum(expo, axis=-1, keepdims=True)))
    context = jnp.einsum('hqk,khd->qhd', probs, v_heads, precision=lax.Precision.HIGHEST)
    return context.reshape(SEQ, D)

def forward(floated, w_qkv, b_qv, w_out, b_out, gain_one, shift_one, w_up, b_up, w_down, b_down, gain_two, shift_two, seq_lens):
    high = lax.Precision.HIGHEST
    proj = jnp.dot(floated, w_qkv.reshape(D, 3 * D), precision=high)
    query = low_back(low(proj[:, :D] + b_qv[0]))
    keyed = low_back(low(proj[:, D:2 * D]))
    valued = low_back(low(proj[:, 2 * D:] + b_qv[1]))
    stacked = (query.reshape(N_DP, SEQ, D), keyed.reshape(N_DP, SEQ, D), valued.reshape(N_DP, SEQ, D), seq_lens)
    context = lax.map(jax.checkpoint(attend_group), stacked).reshape(TOKENS, D)
    context = low_back(low(context))
    attn = low_back(jnp.dot(context, w_out.T, precision=high))
    y_one = norm_rows(attn + b_out + floated, gain_one, shift_one)
    pre = low_back(jnp.dot(low(y_one), w_up, precision=high) + b_up)
    act = low(jax.nn.gelu(pre, approximate=False))
    ffn = low_back(jnp.dot(act, w_down.T, precision=high))
    return norm_rows(ffn + b_down + y_one, gain_two, shift_two)

def reference(layer_in, seq_lens, w_qkv, b_qv, w_out, b_out, gain_one, shift_one, w_up, b_up, w_down, b_down, gain_two, shift_two, cotangent):
    floats = tuple((a.astype(jnp.float32) for a in (layer_in, w_qkv, b_qv, w_out, b_out, gain_one, shift_one, w_up, b_up, w_down, b_down, gain_two, shift_two)))

    def closed(*values):
        return forward(*values, seq_lens)
    output, pullback = jax.vjp(closed, *floats)
    grads = pullback(cotangent.astype(jnp.float32))
    return (output.astype(jnp.bfloat16), grads[0].astype(jnp.bfloat16), grads[1], grads[2], grads[3], grads[4], grads[5], grads[6], grads[7], grads[8], grads[9], grads[10], grads[11], grads[12])
```

```python
import functools
import math

import jax
import jax.numpy as jnp
from jax import lax
from jax.experimental import pallas as pl
from jax.experimental.pallas import tpu as pltpu
from jax.sharding import PartitionSpec as P

HEAD_DIM = 64
PAIR = 2 * HEAD_DIM
EPS = 1e-05
NEG = -1e30
F32 = jnp.float32
BF16 = jnp.bfloat16
VMEM_LIMIT = 60 << 20


def dot(left, right, left_dim=1, right_dim=0):
    return lax.dot_general(
        left, right, (((left_dim,), (right_dim,)), ((), ())), preferred_element_type=F32
    )


def params(**more):
    return pltpu.CompilerParams(vmem_limit_bytes=VMEM_LIMIT, **more)


def cost(flops, size, trans=0):
    return pl.CostEstimate(flops=int(flops), bytes_accessed=int(size), transcendentals=int(trans))


WHOLE = pl.BlockSpec(memory_space=pltpu.VMEM)
SCALARS = pl.BlockSpec(memory_space=pltpu.SMEM)
LEFT = pl.BlockSpec(memory_space=pl.ANY)


def swap(value):
    return lax.ppermute(value, "tensor", [(0, 1), (1, 0)])


def hop(value, step):
    return lax.ppermute(value, "dp", [(i, i ^ step) for i in range(lax.axis_size("dp"))])


def by_hops():
    return lax.axis_size("dp") == 16


def row_blocks():
    if by_hops():
        return lax.axis_index("dp").astype(jnp.int32) ^ jnp.arange(16, dtype=jnp.int32)
    return jnp.zeros((1,), jnp.int32)


def gather_rows(shard, cut):
    first, second = shard[:, :cut], shard[:, cut:]
    if not by_hops():
        return [
            lax.all_gather(first, "dp", axis=0, tiled=True)[None],
            lax.all_gather(second, "dp", axis=0, tiled=True)[None],
        ]
    first = jnp.stack([first] + [hop(first, s) for s in (1, 2, 3)])
    second = jnp.stack([second] + [hop(second, s) for s in (4, 8, 12)])
    return (
        [first]
        + [hop(first, s) for s in (4, 8, 12)]
        + [second]
        + [hop(second, s) for s in (1, 2, 3)]
    )


def piece_places(count):
    if count == 2:
        return [(0, [0]), (1, [0])]
    places = [(0, [4 * z + s for s in range(4)]) for z in range(4)]
    return places + [(1, [4 * z + s for z in range(4)]) for s in range(4)]


def scatter_rows(pieces):
    if not by_hops():
        return jnp.concatenate(
            [
                lax.psum_scatter(piece[0].astype(F32), "dp", scatter_dimension=0, tiled=True)
                for piece in pieces
            ],
            axis=1,
        )

    def total(parts):
        return functools.reduce(lambda a, b: a + b, [part.astype(F32) for part in parts])

    first = [pieces[0]] + [hop(pieces[z], 4 * z) for z in (1, 2, 3)]
    second = [pieces[4]] + [hop(pieces[4 + s], s) for s in (1, 2, 3)]
    first, second = total(first).astype(BF16), total(second).astype(BF16)
    first = [first[0]] + [hop(first[s], s) for s in (1, 2, 3)]
    second = [second[0]] + [hop(second[z], 4 * z) for z in (1, 2, 3)]
    return jnp.concatenate([total(first), total(second)], axis=1)


def sum_dp(value):
    if not by_hops():
        return lax.psum(value, "dp")
    for steps in ((1, 2, 3), (4, 8, 12)):
        one, two, three = [hop(value, s) for s in steps]
        value = (value + one) + (two + three)
    return value


def load_weight(blocks, pieces, whole, cut, sems, base):
    copies = []
    columns = whole.shape[1]
    for piece, (side, places) in zip(pieces, piece_places(len(pieces))):
        rows = piece.shape[1]
        start, size = (0, cut) if side == 0 else (cut, columns - cut)
        for sub, place in enumerate(places):
            at = pl.multiple_of(blocks[place] * rows, 16)
            copies.append(
                pltpu.make_async_copy(
                    piece.at[sub],
                    whole.at[pl.ds(at, rows), pl.ds(start, size)],
                    sems.at[base + len(copies)],
                )
            )
    return copies


def store_pieces(blocks, outs, column, tile):
    cut = outs[0].shape[2]
    side_now = 0 if column < cut else 1
    for out, (side, places) in zip(outs, piece_places(len(outs))):
        if side != side_now:
            continue
        rows = out.shape[1]
        start = column - side * cut
        for sub, place in enumerate(places):
            at = pl.multiple_of(blocks[place] * rows, 16)
            out[sub, :, start : start + tile.shape[1]] = tile[pl.ds(at, rows), :]


def piece_shapes(blocks, rows, cut, columns):
    if blocks == 1:
        return [
            jax.ShapeDtypeStruct((1, rows, cut), BF16),
            jax.ShapeDtypeStruct((1, rows, columns - cut), BF16),
        ]
    return [jax.ShapeDtypeStruct((4, rows // 16, cut), BF16)] * 4 + [
        jax.ShapeDtypeStruct((4, rows // 16, columns - cut), BF16)
    ] * 4


def head_rows(shape, head):
    row = lax.broadcasted_iota(jnp.int32, shape, 0)
    return (row >= head * HEAD_DIM) & (row < (head + 1) * HEAD_DIM)


def attend_kernel(count, cut, blocks, own, oth, bias, extra, *rest):
    pieces = rest[:count]
    q_out, k_out, v_out, ctx_a, ctx_b, ctx_t, lse_out = rest[count : count + 7]
    weight, proj, sems = rest[count + 7 :]
    pair = pl.program_id(0)
    half = weight.shape[1] // 3
    rows = own.shape[0]

    @pl.when(pair == 0)
    def _():
        copies = load_weight(blocks, pieces, weight, cut, sems, 0)
        for copy in copies:
            copy.start()
        for copy in copies:
            copy.wait()
        for place, ref in enumerate((own, oth)):
            proj[place * rows : (place + 1) * rows, :] = (
                dot(ref[...], weight[...]) + bias[...]
            ).astype(BF16)

    def columns(kind):
        return proj[:, pl.ds(pl.multiple_of(kind * half + pair * PAIR, PAIR), PAIR)]

    query, keyed, valued = columns(0), columns(1), columns(2)
    seq = query.shape[0]
    k_out[...] = keyed
    v_out[...] = valued
    q_t = (query.astype(F32) * HEAD_DIM**-0.5).T
    q_out[...] = q_t.astype(BF16)
    v_t = valued.astype(F32).T
    k_aug = jnp.concatenate([keyed, extra[...]], axis=1)
    tail_row = lax.broadcasted_iota(jnp.int32, (PAIR, seq), 0)
    tail = jnp.where(tail_row == 3, 1.0, 0.0).astype(BF16)
    step = min(256, seq)
    for head in range(2):
        mine = head_rows((PAIR, seq), head)
        q_aug = jnp.concatenate([jnp.where(mine, q_t, 0.0).astype(BF16), tail], axis=0)
        v_aug = jnp.where(mine, v_t, 1.0).astype(BF16)
        for at in range(0, seq, step):
            scores = dot(k_aug, q_aug[:, at : at + step])
            top = jnp.max(scores, axis=0, keepdims=True)
            expo = jnp.exp(scores - top).astype(BF16)
            both = dot(v_aug, expo)
            own_at, oth_at = head * HEAD_DIM, (1 - head) * HEAD_DIM
            total = both[oth_at : oth_at + HEAD_DIM]
            ctx_t[own_at : own_at + HEAD_DIM, at : at + step] = (
                both[own_at : own_at + HEAD_DIM] / total
            ).astype(BF16)
            lse_out[0, head : head + 1, at : at + step] = top + jnp.log(total[0:1])
    turned = ctx_t[...].astype(F32).T.astype(BF16)
    ctx_a[...] = turned[:rows]
    ctx_b[...] = turned[rows:]


def attend(blocks, own, oth, bias, extra, pieces, cut):
    rows, width = own.shape
    seq = 2 * rows
    columns = bias.shape[1]
    half = columns // 3
    pairs = half // PAIR
    wide = pl.BlockSpec((PAIR, seq), lambda p: (p, 0))
    tall = pl.BlockSpec((seq, PAIR), lambda p: (0, p))
    tall_half = pl.BlockSpec((rows, PAIR), lambda p: (0, p))
    shape = jax.ShapeDtypeStruct
    return pl.pallas_call(
        functools.partial(attend_kernel, len(pieces), cut),
        grid=(pairs,),
        in_specs=[SCALARS, WHOLE, WHOLE, WHOLE, WHOLE] + [LEFT] * len(pieces),
        out_specs=[
            wide,
            tall,
            tall,
            tall_half,
            tall_half,
            wide,
            pl.BlockSpec((1, 8, seq), lambda p: (p, 0, 0)),
        ],
        out_shape=[
            shape((half, seq), BF16),
            shape((seq, half), BF16),
            shape((seq, half), BF16),
            shape((rows, half), BF16),
            shape((rows, half), BF16),
            shape((half, seq), BF16),
            shape((pairs, 8, seq), F32),
        ],
        scratch_shapes=[
            pltpu.VMEM((width, columns), BF16),
            pltpu.VMEM((seq, columns), BF16),
            pltpu.SemaphoreType.DMA((32,)),
        ],
        compiler_params=params(),
        cost_estimate=cost(
            2 * seq * width * columns + 16 * pairs * seq * seq * PAIR, 12 << 20, seq * seq * 2 * pairs
        ),
        name="attend",
    )(blocks, own, oth, bias, extra, *pieces)


def three_parts(value):
    high = value.astype(BF16).astype(F32)
    mid = (value - high).astype(BF16).astype(F32)
    return high, mid, value - high - mid


def attend_back_kernel(q_t, keyed, valued, ctx_t, lse, d_a, d_b, extra, dq, dk, dv, sums, d_qt):
    seq = keyed.shape[0]
    tail_row = lax.broadcasted_iota(jnp.int32, (PAIR, seq), 0)

    def tail(parts, mask):
        rows = jnp.where(tail_row == 3, mask, 0.0)
        for place, part in enumerate(parts):
            rows = jnp.where(tail_row == place, part, rows)
        return rows.astype(BF16)

    d_t = jnp.concatenate([d_a[...].astype(F32).T, d_b[...].astype(F32).T], axis=1)
    q_full = q_t[...].astype(F32)
    product = d_t * ctx_t[...].astype(F32)
    k_aug = jnp.concatenate([keyed[...], extra[...]], axis=1)
    v_aug = jnp.concatenate([valued[...], extra[...]], axis=1)
    k_t = keyed[...].astype(F32).T.astype(BF16)
    step = min(256, seq)
    q_heads, d_heads, q_augs, d_augs = [], [], [], []
    for head in range(2):
        mine = head_rows((PAIR, seq), head)
        delta = jnp.sum(
            product[head * HEAD_DIM : (head + 1) * HEAD_DIM], axis=0, keepdims=True
        )
        q_heads.append(jnp.where(mine, q_full, 0.0).astype(BF16))
        d_heads.append(jnp.where(mine, d_t, 0.0).astype(BF16))
        q_augs.append(
            jnp.concatenate([q_heads[head], tail(three_parts(-lse[0, head : head + 1, :]), 1.0)], axis=0)
        )
        d_augs.append(jnp.concatenate([d_heads[head], tail(three_parts(-delta), 0.0)], axis=0))
    for at in range(0, seq, step):
        keys = slice(at, at + step)
        key_sum = value_sum = None
        for head in range(2):
            probs = jnp.exp(dot(k_aug[keys], q_augs[head]))
            d_probs = dot(v_aug[keys], d_augs[head])
            d_scores = (probs * d_probs).astype(BF16)
            part = dot(probs.astype(BF16), d_heads[head], 1, 1)
            value_sum = part if head == 0 else value_sum + part
            part = dot(d_scores, q_heads[head], 1, 1)
            key_sum = part if head == 0 else key_sum + part
            lines = slice(head * HEAD_DIM, (head + 1) * HEAD_DIM)
            part = dot(k_t[lines, keys], d_scores)
            if at == 0:
                d_qt[lines, :] = part
            else:
                d_qt[lines, :] += part
        dk[keys, :] = key_sum.astype(BF16)
        dv[keys, :] = value_sum.astype(BF16)
    dq[...] = (d_qt[...] * HEAD_DIM**-0.5).T.astype(BF16)
    sums[0] = jnp.zeros(sums.shape[1:], F32)
    sums[0, 0:1, :] = jnp.sum(dq[...].astype(F32), axis=0, keepdims=True)
    sums[0, 1:2, :] = jnp.sum(dv[...].astype(F32), axis=0, keepdims=True)


def attend_back(q_t, keyed, valued, ctx_t, lse, d_a, d_b, extra):
    seq, half = keyed.shape
    pairs = half // PAIR
    wide = pl.BlockSpec((PAIR, seq), lambda p: (p, 0))
    tall = pl.BlockSpec((seq, PAIR), lambda p: (0, p))
    tall_half = pl.BlockSpec((seq // 2, PAIR), lambda p: (0, p))
    shape = jax.ShapeDtypeStruct
    return pl.pallas_call(
        attend_back_kernel,
        grid=(pairs,),
        in_specs=[
            wide,
            tall,
            tall,
            wide,
            pl.BlockSpec((1, 8, seq), lambda p: (p, 0, 0)),
            tall_half,
            tall_half,
            WHOLE,
        ],
        out_specs=[tall, tall, tall, pl.BlockSpec((1, 8, PAIR), lambda p: (p, 0, 0))],
        out_shape=[shape((seq, half), BF16)] * 3 + [shape((pairs, 8, PAIR), F32)],
        scratch_shapes=[pltpu.VMEM((PAIR, seq), F32)],
        compiler_params=params(),
        cost_estimate=cost(40 * pairs * seq * seq * PAIR, 8 << 20, seq * seq * 2 * pairs),
        name="attend_back",
    )(q_t, keyed, valued, ctx_t, lse, d_a, d_b, extra)


def row_mean(value):
    return jnp.mean(value, axis=1, keepdims=True)


def normed(value):
    centred = value - row_mean(value)
    rate = lax.rsqrt(row_mean(centred * centred) + EPS)
    return centred * rate, rate


def norm_back(grad, hat, rate, gain):
    scaled = grad * gain
    return rate * (scaled - row_mean(scaled) - hat * row_mean(scaled * hat))


def column_sum(value):
    return jnp.sum(value, axis=0, keepdims=True)


def middle_kernel(count, cut, blocks, ctx_own, ctx_oth, x_ref, cot_ref, vectors, b_up, *rest):
    pieces = (rest[:count], rest[count : 2 * count])
    outs = rest[2 * count : 2 * count + 10]
    out, y_low, d_low, dz_low, dz, act_out, dpre_out, dctx_own, dctx_oth, sums = outs
    w_own, w_oth, act_s, slope_s, sems = rest[2 * count + 10 :]
    weights = (w_own, w_oth)
    step = pl.program_id(0)
    half = ctx_own.shape[1]
    hidden = (w_own.shape[1] - half) // 2
    width = x_ref.shape[1]

    @pl.when(step == 0)
    def _():
        copies = []
        for side in range(2):
            copies += load_weight(blocks, pieces[side], weights[side], cut, sems, len(copies))
        for copy in copies:
            copy.start()
        for copy in copies:
            copy.wait()
        sums[...] = jnp.zeros_like(sums)

    b_out, gain_one, shift_one = vectors[0:1, :], vectors[1:2, :], vectors[2:3, :]
    b_down, gain_two, shift_two = vectors[3:4, :], vectors[4:5, :], vectors[5:6, :]

    attn = dot(ctx_own[...], w_own[:, :half], 1, 1) + dot(ctx_oth[...], w_oth[:, :half], 1, 1)
    z_one = attn + b_out + x_ref[...].astype(F32)
    hat_one, rate_one = normed(z_one)
    y_one = hat_one * gain_one + shift_one
    low = y_one.astype(BF16)
    y_low[...] = low
    chunk = 512
    spans = [(side, at) for side in range(2) for at in range(0, hidden, chunk)]
    ffn = None
    for side, at in spans:
        up = weights[side][:, half + at : half + at + chunk]
        place = side * hidden + at
        pre = dot(low, up) + b_up[side : side + 1, at : at + chunk]
        phi = 0.5 + 0.5 * lax.erf(pre * (0.5**0.5))
        act = (pre * phi).astype(BF16)
        slope = phi + pre * jnp.exp(pre * pre * -0.5) * (1.0 / math.sqrt(2.0 * math.pi))
        act_out[:, place : place + chunk] = act
        slope_s[:, place : place + chunk] = slope.astype(BF16)
        down = weights[side][:, half + hidden + at : half + hidden + at + chunk]
        part = dot(act, down, 1, 1)
        ffn = part if ffn is None else ffn + part
    hat_two, rate_two = normed(ffn + b_down + y_one)
    out[...] = (hat_two * gain_two + shift_two).astype(BF16)
    cot = cot_ref[...].astype(F32)
    d_two = norm_back(cot, hat_two, rate_two, gain_two)
    d_ffn = d_two.astype(BF16)
    d_low[...] = d_ffn
    back = None
    for side, at in spans:
        place = side * hidden + at
        down = weights[side][:, half + hidden + at : half + hidden + at + chunk]
        slope = slope_s[:, place : place + chunk].astype(F32)
        d_pre = (dot(d_ffn, down) * slope).astype(BF16)
        dpre_out[:, place : place + chunk] = d_pre
        row = 6 + place // width
        total = column_sum(d_pre.astype(F32))
        for col in range(0, chunk, 256):
            spot = place + col
            sums[6 + spot // width : 7 + spot // width, spot % width : spot % width + 256] += total[
                :, col : col + 256
            ]
        up = weights[side][:, half + at : half + at + chunk]
        part = dot(d_pre, up, 1, 1)
        back = part if back is None else back + part
    d_one = d_two + back
    d_zero = norm_back(d_one, hat_one, rate_one, gain_one)
    dz[...] = d_zero
    d_attn = d_zero.astype(BF16)
    dz_low[...] = d_attn
    dctx_own[...] = dot(d_attn, w_own[:, :half]).astype(BF16)
    dctx_oth[...] = dot(d_attn, w_oth[:, :half]).astype(BF16)
    for row, value in enumerate(
        (d_zero, d_one * hat_one, d_one, d_two, cot * hat_two, cot)
    ):
        sums[row : row + 1, :] += column_sum(value)


def middle(blocks, ctx_own, ctx_oth, own, cotangent, vectors, b_up, own_pieces, oth_pieces, cut):
    rows, width = own.shape
    half = ctx_own.shape[1]
    hidden = b_up.shape[1]
    columns = half + 2 * hidden
    block = min(256, rows)

    def spec(size):
        return pl.BlockSpec((block, size), lambda i: (i, 0))

    shape = jax.ShapeDtypeStruct
    count = len(own_pieces)
    sum_rows = 6 + 2 * hidden // width
    flops = 4 * rows * width * (2 * half) + 8 * rows * width * 2 * hidden
    return pl.pallas_call(
        functools.partial(middle_kernel, count, cut),
        grid=(rows // block,),
        in_specs=[SCALARS, spec(half), spec(half), spec(width), spec(width), WHOLE, WHOLE]
        + [LEFT] * (2 * count),
        out_specs=[
            spec(width),
            spec(width),
            spec(width),
            spec(width),
            spec(width),
            spec(2 * hidden),
            spec(2 * hidden),
            spec(half),
            spec(half),
            pl.BlockSpec((sum_rows, width), lambda i: (0, 0)),
        ],
        out_shape=[
            shape((rows, width), BF16),
            shape((rows, width), BF16),
            shape((rows, width), BF16),
            shape((rows, width), BF16),
            shape((rows, width), F32),
            shape((rows, 2 * hidden), BF16),
            shape((rows, 2 * hidden), BF16),
            shape((rows, half), BF16),
            shape((rows, half), BF16),
            shape((sum_rows, width), F32),
        ],
        scratch_shapes=[
            pltpu.VMEM((width, columns), BF16),
            pltpu.VMEM((width, columns), BF16),
            pltpu.VMEM((8, 128), BF16),
            pltpu.VMEM((block, 2 * hidden), BF16),
            pltpu.SemaphoreType.DMA((64,)),
        ],
        compiler_params=params(),
        cost_estimate=cost(flops, 24 << 20, rows * hidden * 4),
        name="middle",
    )(blocks, ctx_own, ctx_oth, own, cotangent, vectors, b_up, *own_pieces, *oth_pieces)


def grad_tiles(half, hidden):
    tiles = [(0, 0, 0)]
    for which in (1, 2):
        for at in range(0, hidden, half):
            tiles.append((half + (which - 1) * hidden + at, which, at))
    return tiles


def grad_send_kernel(dz_low, ctx, y_low, d_pre, d_low, act, out):
    half = ctx.shape[1]
    hidden = (out.shape[1] - half) // 2
    lefts = (dz_low, y_low, d_low)
    rights = (ctx, d_pre, act)
    for column, which, at in grad_tiles(half, hidden):
        out[:, column : column + half] = dot(
            lefts[which][...], rights[which][:, at : at + half], 0, 0
        ).astype(BF16)


def grad_keep_kernel(blocks, dz_low, ctx, y_low, d_pre, d_low, act, received, *rest):
    outs, tile = rest[:-1], rest[-1]
    half = ctx.shape[1]
    hidden = (received.shape[1] - half) // 2
    lefts = (dz_low, y_low, d_low)
    rights = (ctx, d_pre, act)
    for column, which, at in grad_tiles(half, hidden):
        tile[...] = (
            dot(lefts[which][...], rights[which][:, at : at + half], 0, 0)
            + received[:, column : column + half].astype(F32)
        ).astype(BF16)
        store_pieces(blocks, outs, column, tile)


def half_columns(rows, hidden, side):
    return pl.BlockSpec((rows, hidden), lambda i, side=side: (0, side))


def grads(blocks, dz_low, ctx_own, ctx_oth, y_low, d_pre, d_low, act, cut):
    rows, width = y_low.shape
    half = ctx_own.shape[1]
    hidden = act.shape[1] // 2
    columns = half + 2 * hidden
    flops = 2 * rows * width * columns
    shape = jax.ShapeDtypeStruct
    sent = pl.pallas_call(
        grad_send_kernel,
        grid=(1,),
        in_specs=[WHOLE, WHOLE, WHOLE, half_columns(rows, hidden, 1), WHOLE, half_columns(rows, hidden, 1)],
        out_specs=WHOLE,
        out_shape=shape((width, columns), BF16),
        compiler_params=params(),
        cost_estimate=cost(flops, 12 << 20),
        name="grad_send",
    )(dz_low, ctx_oth, y_low, d_pre, d_low, act)
    received = swap(sent)
    shapes = piece_shapes(blocks.shape[0], width, cut, columns)
    return pl.pallas_call(
        grad_keep_kernel,
        grid=(1,),
        in_specs=[
            SCALARS,
            WHOLE,
            WHOLE,
            WHOLE,
            half_columns(rows, hidden, 0),
            WHOLE,
            half_columns(rows, hidden, 0),
            WHOLE,
        ],
        out_specs=[WHOLE] * len(shapes),
        out_shape=shapes,
        scratch_shapes=[pltpu.VMEM((width, half), BF16)],
        compiler_params=params(),
        cost_estimate=cost(flops, 18 << 20),
        name="grad_keep",
    )(blocks, dz_low, ctx_own, y_low, d_pre, d_low, act, received)


def grad_qkv_kernel(blocks, own, oth, dq, dk, dv, *rest):
    outs, tile = rest[:-1], rest[-1]
    rows = own.shape[0]
    half = dq.shape[1]
    for kind, ref in enumerate((dq, dk, dv)):
        tile[...] = (
            dot(own[...], ref[:rows, :], 0, 0) + dot(oth[...], ref[rows:, :], 0, 0)
        ).astype(BF16)
        store_pieces(blocks, outs, kind * half, tile)


def grad_qkv_pieces(blocks, own, oth, dq, dk, dv, cut):
    rows, width = own.shape
    half = dq.shape[1]
    shapes = piece_shapes(blocks.shape[0], width, cut, 3 * half)
    return pl.pallas_call(
        grad_qkv_kernel,
        in_specs=[SCALARS] + [WHOLE] * 5,
        out_specs=[WHOLE] * len(shapes),
        out_shape=shapes,
        scratch_shapes=[pltpu.VMEM((width, half), BF16)],
        compiler_params=params(),
        cost_estimate=cost(12 * rows * width * half, 6 << 20),
        name="grad_qkv",
    )(blocks, own, oth, dq, dk, dv)


def input_kernel(count, cut, blocks, dq, dk, dv, dz, *rest):
    pieces = rest[:count]
    kept, sent, weight, sems = rest[count:]
    copies = load_weight(blocks, pieces, weight, cut, sems, 0)
    for copy in copies:
        copy.start()
    for copy in copies:
        copy.wait()
    rows = kept.shape[0]
    half = dq.shape[1]
    for place in (1, 0):
        total = None
        for kind, ref in enumerate((dq, dk, dv)):
            part = dot(
                ref[place * rows : (place + 1) * rows, :],
                weight[:, kind * half : (kind + 1) * half],
                1,
                1,
            )
            total = part if total is None else total + part
        if place == 1:
            sent[...] = total.astype(BF16)
        else:
            kept[...] = total + dz[...]


def input_grad(blocks, dq, dk, dv, dz, pieces, cut):
    rows, width = dz.shape
    half = dq.shape[1]
    shape = jax.ShapeDtypeStruct
    kept, sent = pl.pallas_call(
        functools.partial(input_kernel, len(pieces), cut),
        in_specs=[SCALARS] + [WHOLE] * 4 + [LEFT] * len(pieces),
        out_specs=[WHOLE] * 2,
        out_shape=[shape((rows, width), F32), shape((rows, width), BF16)],
        scratch_shapes=[
            pltpu.VMEM((width, 3 * half), BF16),
            pltpu.SemaphoreType.DMA((32,)),
        ],
        compiler_params=params(),
        cost_estimate=cost(12 * rows * width * half, 8 << 20),
        name="input_grad",
    )(blocks, dq, dk, dv, dz, *pieces)
    return (kept + swap(sent).astype(F32)).astype(BF16)


def per_device(
    layer_in,
    seq_lens,
    w_qkv,
    b_qv,
    w_out,
    b_out,
    gain_one,
    shift_one,
    w_up,
    b_up,
    w_down,
    b_down,
    gain_two,
    shift_two,
    cotangent,
):
    rows, width = layer_in.shape
    seq = 2 * rows
    side = lax.axis_index("tensor")
    shard_rows, _, half = w_qkv.shape
    hidden = w_up.shape[1]
    blocks = row_blocks()
    cut_qkv = half
    cut_all = 3 * half

    oth_in = swap(layer_in)
    qkv_pieces = gather_rows(w_qkv.reshape(shard_rows, 3 * half), cut_qkv)
    own_pieces = gather_rows(jnp.concatenate([w_out, w_up, w_down], axis=1), cut_all)
    oth_pieces = [swap(piece) for piece in own_pieces]

    bias_qv = lax.dynamic_slice_in_dim(b_qv, side * half, half, 1)
    bias = jnp.concatenate([bias_qv[0:1], jnp.zeros((1, half), F32), bias_qv[1:2]], axis=1)
    row = jnp.arange(seq, dtype=jnp.int32)
    position = ((row // rows) ^ side) * rows + row % rows
    lane = jnp.arange(PAIR, dtype=jnp.int32)[None, :]
    masked = jnp.where(position < seq_lens[0], 0.0, NEG)[:, None]
    extra = jnp.where(lane < 3, 1.0, jnp.where(lane == 3, masked, 0.0)).astype(BF16)

    q_t, keyed, valued, ctx_a, ctx_b, ctx_t, lse = attend(
        blocks, layer_in, oth_in, bias, extra, qkv_pieces, cut_qkv
    )
    ctx_oth = swap(ctx_b)
    up_parts = b_up.reshape(2, hidden)
    up_bias = jnp.where(side == 0, up_parts, up_parts[::-1])
    vectors = jnp.stack([b_out, gain_one, shift_one, b_down, gain_two, shift_two])
    (output, y_low, d_low, dz_low, dz, act, d_pre, dctx_own, dctx_oth, sums) = middle(
        blocks, ctx_a, ctx_oth, layer_in, cotangent, vectors, up_bias, own_pieces, oth_pieces, cut_all
    )
    d_ctx_b = swap(dctx_oth)
    all_pieces = grads(blocks, dz_low, ctx_a, ctx_oth, y_low, d_pre, d_low, act, cut_all)
    grad_all = scatter_rows(all_pieces)

    up_rows = hidden // width
    own_sums = sums[: 6 + up_rows]
    sent_sums = jnp.concatenate([sums[:6], sums[6 + up_rows :]], axis=0)
    totals = sum_dp(own_sums + swap(sent_sums))

    dq, dk, dv, qv_sums = attend_back(q_t, keyed, valued, ctx_t, lse, dctx_own, d_ctx_b, extra)
    qkv_grads = grad_qkv_pieces(blocks, layer_in, oth_in, dq, dk, dv, cut_qkv)
    grad_qkv = scatter_rows(qkv_grads).reshape(shard_rows, 3, half)
    qv = sum_dp(qv_sums[:, :2, :])
    grad_bqv = qv.transpose(1, 0, 2).reshape(2, half)
    grad_input = input_grad(blocks, dq, dk, dv, dz, qkv_pieces, cut_qkv)

    return (
        output,
        grad_input,
        grad_qkv,
        grad_bqv,
        grad_all[:, :half],
        totals[0],
        totals[1],
        totals[2],
        grad_all[:, half : half + hidden],
        totals[6:].reshape(hidden),
        grad_all[:, half + hidden :],
        totals[3],
        totals[4],
        totals[5],
    )


def solution(mesh):
    placed = (
        P(("dp", "tensor"), None),
        P("dp"),
        P("dp", None, "tensor"),
        P(),
        P("dp", "tensor"),
        P(),
        P(),
        P(),
        P("dp", "tensor"),
        P(),
        P("dp", "tensor"),
        P(),
        P(),
        P(),
        P(("dp", "tensor"), None),
    )
    return jax.shard_map(
        per_device,
        mesh=mesh,
        in_specs=placed,
        out_specs=(
            P(("dp", "tensor"), None),
            P(("dp", "tensor"), None),
            P("dp", None, "tensor"),
            P(None, "tensor"),
            P("dp", "tensor"),
            P(),
            P(),
            P(),
            P("dp", "tensor"),
            P("tensor"),
            P("dp", "tensor"),
            P(),
            P(),
            P(),
        ),
        check_vma=False,
    )
```

```python
import functools
import math

import jax
import jax.numpy as jnp
from jax import lax
from jax.experimental import pallas as pl
from jax.experimental.pallas import tpu as pltpu
from jax.sharding import PartitionSpec as P

HEAD_DIM = 64
PAIR = 2 * HEAD_DIM
EPS = 1e-05
NEG = -1e30
F32 = jnp.float32
BF16 = jnp.bfloat16
VMEM_LIMIT = 60 << 20


def dot(left, right, left_dim=1, right_dim=0):
    return lax.dot_general(
        left, right, (((left_dim,), (right_dim,)), ((), ())), preferred_element_type=F32
    )


def params(**more):
    return pltpu.CompilerParams(vmem_limit_bytes=VMEM_LIMIT, **more)


def cost(flops, size, trans=0):
    return pl.CostEstimate(flops=int(flops), bytes_accessed=int(size), transcendentals=int(trans))


WHOLE = pl.BlockSpec(memory_space=pltpu.VMEM)
SCALARS = pl.BlockSpec(memory_space=pltpu.SMEM)
LEFT = pl.BlockSpec(memory_space=pl.ANY)


def swap(value):
    return lax.ppermute(value, "tensor", [(0, 1), (1, 0)])


def by_hops():
    return lax.axis_size("dp") == 16


ORDERS = ((8, 4, 1, 2), (2, 8, 4, 1))


def offsets(core):
    found = [0]
    for step in ORDERS[core]:
        found += [one ^ step for one in found]
    return found


def hop(value, level):
    pairs = [
        (2 * device + core, 2 * (device ^ ORDERS[core][level]) + core)
        for device in range(16)
        for core in range(2)
    ]
    return lax.ppermute(value, ("dp", "tensor"), pairs)


def row_blocks(side):
    if not by_hops():
        return jnp.zeros((2, 1), jnp.int32)
    table = jnp.array([offsets(0), offsets(1)], jnp.int32)
    return lax.axis_index("dp").astype(jnp.int32) ^ jnp.where(side == 0, table, table[::-1])


def after(value, *others):
    return lax.optimization_barrier((value, others))[0] if others else value


class Gather:
    def __init__(self, shard):
        self.held = shard[None]
        self.level = 0

    def step(self, *others):
        held = after(self.held, *others)
        if not by_hops():
            if self.level == 0:
                self.pieces = [lax.all_gather(held[0], "dp", axis=0, tiled=True)[None]]
            self.level += 1
            return self.pieces[0]
        got = hop(held, self.level)
        self.level += 1
        if self.level < 4:
            self.held = jnp.concatenate([held, got], axis=0)
        self.pieces = [held, got]
        return got


class Scatter:
    def __init__(self, pieces, added=False):
        self.parts = list(pieces)
        self.level = 4
        self.added = added

    def total(self, at):
        return functools.reduce(lambda a, b: a + b, [part[at].astype(F32) for part in self.parts])

    def step(self, *others):
        self.level -= 1
        if not by_hops():
            if self.level == 3:
                whole = after(self.parts[0][0], *others).astype(F32)
                if self.added:
                    whole = whole + self.parts[1][0].astype(F32)
                self.sums = lax.psum_scatter(whole, "dp", scatter_dimension=0, tiled=True)
            return self.sums
        if self.level == 3 and not self.added:
            self.parts, sent = self.parts[:1], self.parts[1]
        else:
            size = 1 << self.level
            sent = self.total(slice(size, 2 * size)).astype(BF16)
        got = hop(after(sent, *others), self.level)
        self.parts.append(got)
        return got

    def result(self):
        return self.total(0) if by_hops() else self.sums


class Sum:
    def __init__(self, value):
        self.value = value
        self.level = 0

    def step(self, *others):
        value = after(self.value, *others)
        if by_hops():
            step = ORDERS[0][self.level]
            value = value + lax.ppermute(value, "dp", [(i, i ^ step) for i in range(16)])
        elif self.level == 0:
            value = lax.psum(value, "dp")
        self.value = value
        self.level += 1
        return value


class Mover:
    def __init__(self, sems):
        self.sems = sems
        self.count = 0

    def copy(self, source, target):
        made = pltpu.make_async_copy(source, target, self.sems.at[self.count])
        self.count += 1
        return made

    def start(self, source, target):
        made = self.copy(source, target)
        made.start()
        return made


def wait(copies):
    for copy in copies:
        copy.wait()


def load_weight(mover, blocks, side, pieces, whole, start=0, size=None):
    copies = []
    size = whole.shape[1] if size is None else size
    columns = pl.ds(start, size)
    for piece in pieces:
        rows = piece.shape[1]
        for sub in range(piece.shape[0]):
            at = pl.multiple_of(blocks[side, len(copies)] * rows, 16)
            copies.append(
                mover.copy(piece.at[sub, :, columns], whole.at[pl.ds(at, rows), columns])
            )
    return copies


def store_pieces(blocks, outs, column, tile, side=0):
    place = 0
    for out in outs:
        rows = out.shape[1]
        for sub in range(out.shape[0]):
            at = pl.multiple_of(blocks[side, place] * rows, 16)
            out[sub, :, column : column + tile.shape[1]] = tile[pl.ds(at, rows), :]
            place += 1


def piece_shapes(blocks, rows, columns):
    if blocks == 1:
        return [jax.ShapeDtypeStruct((1, rows, columns), BF16)]
    return [jax.ShapeDtypeStruct((blocks // 2, rows // blocks, columns), BF16)] * 2


def head_rows(shape, head):
    row = lax.broadcasted_iota(jnp.int32, shape, 0)
    return (row >= head * HEAD_DIM) & (row < (head + 1) * HEAD_DIM)


def project_kernel(count, blocks, own, oth, bias, *rest):
    pieces = rest[:count]
    q_out, k_out, v_out, weight, sems = rest[count:]
    half = weight.shape[1] // 3
    rows = own.shape[0]
    copies = load_weight(Mover(sems), blocks, 0, pieces, weight)
    for copy in copies:
        copy.start()
    wait(copies)
    for place, ref in enumerate((own, oth)):
        lines = slice(place * rows, (place + 1) * rows)
        proj = (dot(ref[...], weight[...]) + bias[...]).astype(BF16)
        for at in range(0, half, PAIR):
            q_out[at : at + PAIR, lines] = (
                (proj[:, at : at + PAIR].astype(F32) * HEAD_DIM**-0.5).T.astype(BF16)
            )
        k_out[lines, :] = proj[:, half : 2 * half]
        v_out[lines, :] = proj[:, 2 * half :]


def project(blocks, own, oth, bias, pieces):
    rows, width = own.shape
    seq = 2 * rows
    columns = bias.shape[1]
    half = columns // 3
    shape = jax.ShapeDtypeStruct
    return pl.pallas_call(
        functools.partial(project_kernel, len(pieces)),
        in_specs=[SCALARS, WHOLE, WHOLE, WHOLE] + [LEFT] * len(pieces),
        out_specs=[WHOLE] * 3,
        out_shape=[shape((half, seq), BF16), shape((seq, half), BF16), shape((seq, half), BF16)],
        scratch_shapes=[pltpu.VMEM((width, columns), BF16), pltpu.SemaphoreType.DMA((16,))],
        compiler_params=params(),
        cost_estimate=cost(2 * seq * width * columns, 6 << 20),
        name="project",
    )(blocks, own, oth, bias, *pieces)


def attend_kernel(q_ref, k_ref, v_ref, extra, ctx_a, ctx_b, ctx_t, lse_out):
    rows = ctx_a.shape[0]
    seq = k_ref.shape[0]
    q_t = q_ref[...].astype(F32)
    v_t = v_ref[...].astype(F32).T
    k_aug = jnp.concatenate([k_ref[...], extra[...]], axis=1)
    tail_row = lax.broadcasted_iota(jnp.int32, (PAIR, seq), 0)
    tail = jnp.where(tail_row == 3, 1.0, 0.0).astype(BF16)
    step = min(256, seq)
    for head in range(2):
        mine = head_rows((PAIR, seq), head)
        q_aug = jnp.concatenate([jnp.where(mine, q_t, 0.0).astype(BF16), tail], axis=0)
        v_aug = jnp.where(mine, v_t, 1.0).astype(BF16)
        for at in range(0, seq, step):
            scores = dot(k_aug, q_aug[:, at : at + step])
            top = jnp.max(scores, axis=0, keepdims=True)
            expo = jnp.exp(scores - top).astype(BF16)
            both = dot(v_aug, expo)
            own_at, oth_at = head * HEAD_DIM, (1 - head) * HEAD_DIM
            total = both[oth_at : oth_at + HEAD_DIM]
            ctx_t[own_at : own_at + HEAD_DIM, at : at + step] = (
                both[own_at : own_at + HEAD_DIM] / total
            ).astype(BF16)
            lse_out[head : head + 1, at : at + step] = top + jnp.log(total[0:1])
    turned = ctx_t[...].astype(F32).T.astype(BF16)
    ctx_a[...] = turned[:rows]
    ctx_b[...] = turned[rows:]


def pair_specs(first, seq):
    wide = pl.BlockSpec((PAIR, seq), lambda i: (first + i, 0))
    tall = pl.BlockSpec((seq, PAIR), lambda i: (0, first + i))
    tall_half = pl.BlockSpec((seq // 2, PAIR), lambda i: (0, first + i))
    return wide, tall, tall_half


def attend(first, last, q_t, keyed, valued, extra):
    seq = keyed.shape[0]
    count = last - first
    wide, tall, _ = pair_specs(first, seq)
    own_wide, _, own_half = pair_specs(0, seq)
    shape = jax.ShapeDtypeStruct
    return pl.pallas_call(
        attend_kernel,
        grid=(count,),
        in_specs=[wide, tall, tall, WHOLE],
        out_specs=[own_half, own_half, own_wide, pl.BlockSpec((8, seq), lambda i: (i, 0))],
        out_shape=[
            shape((seq // 2, count * PAIR), BF16),
            shape((seq // 2, count * PAIR), BF16),
            shape((count * PAIR, seq), BF16),
            shape((count * 8, seq), F32),
        ],
        compiler_params=params(),
        cost_estimate=cost(64 * count * seq * seq * PAIR, 2 << 20, count * seq * seq * 2),
        name="attend",
    )(q_t, keyed, valued, extra)


def three_parts(value):
    high = value.astype(BF16).astype(F32)
    mid = (value - high).astype(BF16).astype(F32)
    return high, mid, value - high - mid


def attend_back_kernel(q_t, keyed, valued, ctx_t, lse, d_a, d_b, extra, dq, dk, dv, sums, d_qt):
    seq = keyed.shape[0]
    tail_row = lax.broadcasted_iota(jnp.int32, (PAIR, seq), 0)

    def tail(parts, mask):
        rows = jnp.where(tail_row == 3, mask, 0.0)
        for place, part in enumerate(parts):
            rows = jnp.where(tail_row == place, part, rows)
        return rows.astype(BF16)

    d_t = jnp.concatenate([d_a[...].astype(F32).T, d_b[...].astype(F32).T], axis=1)
    q_full = q_t[...].astype(F32)
    product = d_t * ctx_t[...].astype(F32)
    k_aug = jnp.concatenate([keyed[...], extra[...]], axis=1)
    v_aug = jnp.concatenate([valued[...], extra[...]], axis=1)
    k_t = keyed[...].astype(F32).T.astype(BF16)
    step = min(256, seq)
    q_heads, d_heads, q_augs, d_augs = [], [], [], []
    for head in range(2):
        mine = head_rows((PAIR, seq), head)
        delta = jnp.sum(
            product[head * HEAD_DIM : (head + 1) * HEAD_DIM], axis=0, keepdims=True
        )
        q_heads.append(jnp.where(mine, q_full, 0.0).astype(BF16))
        d_heads.append(jnp.where(mine, d_t, 0.0).astype(BF16))
        q_augs.append(
            jnp.concatenate([q_heads[head], tail(three_parts(-lse[head : head + 1, :]), 1.0)], axis=0)
        )
        d_augs.append(jnp.concatenate([d_heads[head], tail(three_parts(-delta), 0.0)], axis=0))
    for at in range(0, seq, step):
        keys = slice(at, at + step)
        key_sum = value_sum = None
        for head in range(2):
            probs = jnp.exp(dot(k_aug[keys], q_augs[head]))
            d_probs = dot(v_aug[keys], d_augs[head])
            d_scores = (probs * d_probs).astype(BF16)
            part = dot(probs.astype(BF16), d_heads[head], 1, 1)
            value_sum = part if head == 0 else value_sum + part
            part = dot(d_scores, q_heads[head], 1, 1)
            key_sum = part if head == 0 else key_sum + part
            lines = slice(head * HEAD_DIM, (head + 1) * HEAD_DIM)
            part = dot(k_t[lines, keys], d_scores)
            if at == 0:
                d_qt[lines, :] = part
            else:
                d_qt[lines, :] += part
        dk[keys, :] = key_sum.astype(BF16)
        dv[keys, :] = value_sum.astype(BF16)
    dq[...] = (d_qt[...] * HEAD_DIM**-0.5).T.astype(BF16)
    sums[...] = jnp.zeros(sums.shape, F32)
    sums[0:1, :] = jnp.sum(dq[...].astype(F32), axis=0, keepdims=True)
    sums[1:2, :] = jnp.sum(dv[...].astype(F32), axis=0, keepdims=True)


def attend_back(first, last, q_t, keyed, valued, ctx_t, lse, d_a, d_b, extra):
    seq = keyed.shape[0]
    count = last - first
    wide, tall, tall_half = pair_specs(first, seq)
    own_wide, own_tall, _ = pair_specs(0, seq)
    shape = jax.ShapeDtypeStruct
    return pl.pallas_call(
        attend_back_kernel,
        grid=(count,),
        in_specs=[
            wide,
            tall,
            tall,
            own_wide,
            pl.BlockSpec((8, seq), lambda i: (i, 0)),
            tall_half,
            tall_half,
            WHOLE,
        ],
        out_specs=[own_tall] * 3 + [pl.BlockSpec((8, PAIR), lambda i: (0, i))],
        out_shape=[shape((seq, count * PAIR), BF16)] * 3 + [shape((8, count * PAIR), F32)],
        scratch_shapes=[pltpu.VMEM((PAIR, seq), F32)],
        compiler_params=params(),
        cost_estimate=cost(64 * count * seq * seq * PAIR, 3 << 20, count * seq * seq * 2),
        name="attend_back",
    )(q_t, keyed, valued, ctx_t, lse, d_a, d_b, extra)


def row_mean(value):
    return jnp.mean(value, axis=1, keepdims=True)


def normed(value):
    centred = value - row_mean(value)
    rate = lax.rsqrt(row_mean(centred * centred) + EPS)
    return centred * rate, rate


def norm_back(grad, hat, rate, gain):
    scaled = grad * gain
    return rate * (scaled - row_mean(scaled) - hat * row_mean(scaled * hat))


def column_sum(value):
    return jnp.sum(value, axis=0, keepdims=True)


def gelu(value):
    phi = 0.5 + 0.5 * lax.erf(value * (0.5**0.5))
    return phi, jnp.exp(value * value * -0.5) * (1.0 / math.sqrt(2.0 * math.pi))


def hidden_spans(hidden, chunk):
    return [(side, at, side * hidden + at) for side in range(2) for at in range(0, hidden, chunk)]


CHUNK = 512


def middle_kernel(count, parts, blocks, *rest):
    ctx_parts = rest[:parts]
    ctx_oth, x_ref, cot_ref, vectors, b_up = rest[parts : parts + 5]
    rest = rest[parts + 5 :]
    pieces = [rest[at : at + count] for at in range(0, 4 * count, count)]
    rest = rest[4 * count :]
    out, dz, dctx_own, dctx_oth, sums, sent_f, kept_f, sent_d, kept_d = rest[:9]
    w_own, w_oth, down_own, down_oth = rest[9:13]
    ctx_s, x_s, cot_s, act_s, slope_s, y_t, d_t, dz_t = rest[13:21]
    out_s, dz_s, dctx_s, tile, got_f, got_d, sems = rest[21:]
    wholes, downs = (w_own, w_oth), (down_own, down_oth)
    half = ctx_oth.shape[1]
    hidden = down_own.shape[1]
    width = x_ref.shape[1]
    mover = Mover(sems)
    stores = []

    inputs, at = [], 0
    for part in ctx_parts:
        size = part.shape[1]
        inputs.append(mover.start(part, ctx_s.at[0, :, pl.ds(at, size)]))
        at += size
    inputs.append(mover.start(ctx_oth, ctx_s.at[1]))
    loads = []
    for span in ((0, half), (half, hidden)):
        for side in range(2):
            loads.append(load_weight(mover, blocks, side, pieces[side], wholes[side], *span))
    for side in range(2):
        loads.append(load_weight(mover, blocks, side, pieces[2 + side], downs[side]))
    for place, load in enumerate(loads):
        for copy in load:
            copy.start()
        if place == 1:
            inputs.append(mover.start(x_ref, x_s))
    late = mover.start(cot_ref, cot_s)
    wait(inputs + loads[0] + loads[1])

    def put(tiles, lefts, rights, side, held, out_ref):
        for left, right, at, size, column in tiles:
            tile[:, :size] = dot(lefts[left][...], rights[right][:, at : at + size]).astype(BF16)
            store_pieces(blocks, [held], column, tile.at[:, pl.ds(0, size)], side)
            span = pl.ds(column, size)
            stores.append(mover.start(held.at[:, :, span], out_ref.at[:, :, span]))

    b_out, gain_one, shift_one = vectors[0:1, :], vectors[1:2, :], vectors[2:3, :]
    b_down, gain_two, shift_two = vectors[3:4, :], vectors[4:5, :], vectors[5:6, :]
    attn = dot(ctx_s[0], w_own[:, :half], 1, 1) + dot(ctx_s[1], w_oth[:, :half], 1, 1)
    hat_one, rate_one = normed(attn + b_out + x_s[...].astype(F32))
    y_one = hat_one * gain_one + shift_one
    low = y_one.astype(BF16)
    spans = hidden_spans(hidden, CHUNK)
    ffn = None
    for side, at, place in spans:
        if at == 0:
            wait(loads[2 + side])
        pre = dot(low, wholes[side][:, half + at : half + at + CHUNK])
        pre = pre + b_up[side : side + 1, at : at + CHUNK]
        phi, bell = gelu(pre)
        act_s[:, place : place + CHUNK] = (pre * phi).astype(BF16)
        slope_s[:, place : place + CHUNK] = (phi + pre * bell).astype(BF16)
    for side in range(2):
        wait(loads[4 + side])
        part = dot(act_s[:, side * hidden : (side + 1) * hidden], downs[side][...], 1, 1)
        ffn = part if ffn is None else ffn + part
    hat_two, rate_two = normed(ffn + b_down + y_one)
    out_s[...] = (hat_two * gain_two + shift_two).astype(BF16)
    stores.append(mover.start(out_s, out))
    late.wait()
    cot = cot_s[...].astype(F32)
    d_two = norm_back(cot, hat_two, rate_two, gain_two)
    d_ffn = d_two.astype(BF16)
    d_t[...] = d_two.T.astype(BF16)
    y_t[...] = y_one.T.astype(BF16)
    sums[3:4, :] = column_sum(d_two)
    sums[4:5, :] = column_sum(cot * hat_two)
    sums[5:6, :] = column_sum(cot)
    for side, (held, out_ref) in ((1, (got_d.at[1], sent_d)), (0, (got_d.at[0], kept_d))):
        tiles = [(0, 0, side * hidden + at, CHUNK, at) for at in range(0, hidden, CHUNK)]
        put(tiles, [d_t], [act_s], side, held, out_ref)
    back = None
    for side, at, place in spans:
        d_act = dot(d_ffn, downs[side][:, at : at + CHUNK])
        d_pre = (d_act * slope_s[:, place : place + CHUNK].astype(F32)).astype(BF16)
        slope_s[:, place : place + CHUNK] = d_pre
        total = column_sum(d_pre.astype(F32))
        for col in range(0, CHUNK, 256):
            spot = place + col
            row, left = 6 + spot // width, spot % width
            sums[row : row + 1, left : left + 256] = total[:, col : col + 256]
        part = dot(d_pre, wholes[side][:, half + at : half + at + CHUNK], 1, 1)
        back = part if back is None else back + part
    d_one = d_two + back
    d_zero = norm_back(d_one, hat_one, rate_one, gain_one)
    dz_s[...] = d_zero
    stores.append(mover.start(dz_s, dz))
    d_attn = d_zero.astype(BF16)
    dctx_s[0] = dot(d_attn, w_own[:, :half]).astype(BF16)
    dctx_s[1] = dot(d_attn, w_oth[:, :half]).astype(BF16)
    stores.append(mover.start(dctx_s.at[0], dctx_own))
    stores.append(mover.start(dctx_s.at[1], dctx_oth))
    dz_t[...] = d_zero.T.astype(BF16)
    sums[0:1, :] = column_sum(d_zero)
    sums[1:2, :] = column_sum(d_one * hat_one)
    sums[2:3, :] = column_sum(d_one)
    for side, (held, out_ref) in ((1, (got_f.at[1], sent_f)), (0, (got_f.at[0], kept_f))):
        tiles = [
            (1, 1, side * hidden + at, CHUNK, half + at) for at in range(0, hidden, CHUNK)
        ] + [(0, 0, 0, half, 0)]
        put(tiles, [dz_t, y_t], [ctx_s.at[side], slope_s], side, held, out_ref)
    wait(stores)


def middle(blocks, ctx_parts, ctx_oth, own, cotangent, vectors, b_up, pieces):
    rows, width = own.shape
    half = ctx_oth.shape[1]
    hidden = b_up.shape[1]
    shape = jax.ShapeDtypeStruct
    count = len(pieces[0])
    sum_rows = 6 + 2 * hidden // width
    flops = 2 * rows * width * (6 * half + 12 * hidden)
    number = blocks.shape[1]
    first = (number, width // number, half + hidden)
    down = (number, width // number, hidden)
    vmem = pltpu.VMEM
    return pl.pallas_call(
        functools.partial(middle_kernel, count, len(ctx_parts)),
        in_specs=[SCALARS]
        + [LEFT] * (len(ctx_parts) + 3)
        + [WHOLE, WHOLE]
        + [LEFT] * (4 * count),
        out_specs=[LEFT] * 4 + [WHOLE] + [LEFT] * 4,
        out_shape=[
            shape((rows, width), BF16),
            shape((rows, width), F32),
            shape((rows, half), BF16),
            shape((rows, half), BF16),
            shape((sum_rows, width), F32),
            shape(first, BF16),
            shape(first, BF16),
            shape(down, BF16),
            shape(down, BF16),
        ],
        scratch_shapes=[vmem((width, half + hidden), BF16)] * 2
        + [vmem((width, hidden), BF16)] * 2
        + [
            vmem((2, rows, half), BF16),
            vmem((rows, width), BF16),
            vmem((rows, width), BF16),
            vmem((rows, 2 * hidden), BF16),
            vmem((rows, 2 * hidden), BF16),
            vmem((width, rows), BF16),
            vmem((width, rows), BF16),
            vmem((width, rows), BF16),
            vmem((rows, width), BF16),
            vmem((rows, width), F32),
            vmem((2, rows, half), BF16),
            vmem((width, CHUNK), BF16),
            vmem((2, *first), BF16),
            vmem((2, *down), BF16),
            pltpu.SemaphoreType.DMA((144,)),
        ],
        compiler_params=params(),
        cost_estimate=cost(flops, 28 << 20, rows * hidden * 4),
        name="middle",
    )(
        blocks,
        *ctx_parts,
        ctx_oth,
        own,
        cotangent,
        vectors,
        b_up,
        *[piece for group in pieces for piece in group],
    )


def pair_places(parts):
    return [
        (group, at) for group, part in enumerate(parts) for at in range(0, part[0].shape[1], PAIR)
    ]


def grad_qkv_kernel(groups, blocks, x_t, *refs):
    parts = [refs[3 * group : 3 * group + 3] for group in range(groups)]
    refs = refs[3 * groups :]
    x_s, right_s, tile, sems = refs[-4:]
    outs, held = refs[:-6], refs[-6:-4]
    held = held[: len(outs)]
    mover = Mover(sems)
    loads = [mover.start(x_t, x_s)]
    places = pair_places(parts)
    for pair, (group, at) in enumerate(places):
        loads.append(
            [
                mover.start(
                    part.at[:, pl.ds(at, PAIR)], right_s.at[pair, :, pl.ds(kind * PAIR, PAIR)]
                )
                for kind, part in enumerate(parts[group])
            ]
        )
    loads[0].wait()
    stores = []
    for pair in range(len(places)):
        wait(loads[1 + pair])
        tile[...] = dot(x_s[...], right_s[pair]).astype(BF16)
        column = 3 * PAIR * pair
        store_pieces(blocks, held, column, tile)
        span = pl.ds(column, 3 * PAIR)
        for mine, out in zip(held, outs):
            stores.append(mover.start(mine.at[:, :, span], out.at[:, :, span]))
    wait(stores)


def grad_qkv_pieces(blocks, x_t, d_parts):
    width, seq = x_t.shape
    flat = [part for parts in d_parts for part in parts]
    columns = sum(part.shape[1] for part in flat)
    shapes = piece_shapes(blocks.shape[1], width, columns)
    held = [pltpu.VMEM(one.shape, BF16) for one in shapes]
    held += [pltpu.VMEM((8, 128), BF16)] * (2 - len(held))
    return pl.pallas_call(
        functools.partial(grad_qkv_kernel, len(d_parts)),
        in_specs=[SCALARS] + [LEFT] * (1 + len(flat)),
        out_specs=[LEFT] * len(shapes),
        out_shape=shapes,
        scratch_shapes=held
        + [
            pltpu.VMEM((width, seq), BF16),
            pltpu.VMEM((columns // (3 * PAIR), seq, 3 * PAIR), BF16),
            pltpu.VMEM((width, 3 * PAIR), BF16),
            pltpu.SemaphoreType.DMA((32,)),
        ],
        compiler_params=params(),
        cost_estimate=cost(2 * seq * width * columns, 6 << 20),
        name="grad_qkv",
    )(blocks, x_t, *flat)


def input_kernel(count, groups, blocks, *refs):
    parts = [refs[3 * group : 3 * group + 3] for group in range(groups)]
    refs = refs[3 * groups :]
    dz, pieces = refs[0], refs[1 : 1 + count]
    kept, sent, weight, whole, dz_s, sent_s, sems = refs[1 + count :]
    mover = Mover(sems)
    rows = kept.shape[0]
    half = whole.shape[1] // 3
    loads = load_weight(mover, blocks, 0, pieces, weight)
    for pair, (group, at) in enumerate(pair_places(parts)):
        for kind, part in enumerate(parts[group]):
            target = whole.at[:, pl.ds(kind * half + pair * PAIR, PAIR)]
            loads.append(mover.copy(part.at[:, pl.ds(at, PAIR)], target))
    for copy in loads:
        copy.start()
    last = mover.start(dz, dz_s)
    wait(loads)
    sent_s[...] = dot(whole[rows:, :], weight[...], 1, 1).astype(BF16)
    store = mover.start(sent_s, sent)
    last.wait()
    dz_s[...] += dot(whole[:rows, :], weight[...], 1, 1)
    mover.start(dz_s, kept).wait()
    store.wait()


def input_grad(blocks, d_parts, dz, pieces):
    rows, width = dz.shape
    flat = [part for parts in d_parts for part in parts]
    columns = sum(part.shape[1] for part in flat)
    shape = jax.ShapeDtypeStruct
    return pl.pallas_call(
        functools.partial(input_kernel, len(pieces), len(d_parts)),
        in_specs=[SCALARS] + [LEFT] * (len(flat) + 1 + len(pieces)),
        out_specs=[LEFT] * 2,
        out_shape=[shape((rows, width), F32), shape((rows, width), BF16)],
        scratch_shapes=[
            pltpu.VMEM((width, columns), BF16),
            pltpu.VMEM((2 * rows, columns), BF16),
            pltpu.VMEM((rows, width), F32),
            pltpu.VMEM((rows, width), BF16),
            pltpu.SemaphoreType.DMA((48,)),
        ],
        compiler_params=params(),
        cost_estimate=cost(4 * rows * width * columns, 8 << 20),
        name="input_grad",
    )(blocks, *flat, dz, *pieces)


def per_device(
    layer_in,
    seq_lens,
    w_qkv,
    b_qv,
    w_out,
    b_out,
    gain_one,
    shift_one,
    w_up,
    b_up,
    w_down,
    b_down,
    gain_two,
    shift_two,
    cotangent,
):
    rows, width = layer_in.shape
    seq = 2 * rows
    side = lax.axis_index("tensor")
    shard_rows, _, half = w_qkv.shape
    hidden = w_up.shape[1]
    blocks = row_blocks(side)
    pairs = range(half // PAIR)

    gather_qkv = Gather(w_qkv.reshape(shard_rows, 3 * half))
    gather_first = Gather(jnp.concatenate([w_out, w_up], axis=1))
    gather_down = Gather(w_down)
    oth_in = swap(layer_in)
    qkv_0 = gather_qkv.step()
    first_0 = gather_first.step(qkv_0)
    qkv_1 = gather_qkv.step()
    down_0 = gather_down.step(qkv_1)
    qkv_2 = gather_qkv.step()
    first_1 = gather_first.step(qkv_2)
    qkv_3 = gather_qkv.step()
    down_1 = gather_down.step(qkv_3)
    x_t = jnp.concatenate([after(layer_in, qkv_0), oth_in], axis=0).T

    bias_qv = lax.dynamic_slice_in_dim(b_qv, side * half, half, 1)
    bias = jnp.concatenate([bias_qv[0:1], jnp.zeros((1, half), F32), bias_qv[1:2]], axis=1)
    row = jnp.arange(seq, dtype=jnp.int32)
    position = ((row // rows) ^ side) * rows + row % rows
    lane = jnp.arange(PAIR, dtype=jnp.int32)[None, :]
    masked = jnp.where(position < seq_lens[0], 0.0, NEG)[:, None]
    extra = jnp.where(lane < 3, 1.0, jnp.where(lane == 3, masked, 0.0)).astype(BF16)

    q_t, keyed, valued = project(blocks, layer_in, oth_in, bias, gather_qkv.pieces)
    first_2 = gather_first.step(q_t)
    attended = [attend(0, 1, after(q_t, down_1), keyed, valued, extra)]
    gather_first.step(attended[0][3])
    down_2 = gather_down.step(attended[0][3])
    attended.append(attend(1, 2, after(q_t, first_2, attended[0][3]), keyed, valued, extra))
    first_pieces = gather_first.pieces
    gather_down.step(attended[1][3])
    first_oth = [swap(after(first_pieces[0], attended[1][3]))]
    attended.append(attend(2, 3, after(q_t, down_2, attended[1][3]), keyed, valued, extra))
    down_pieces = gather_down.pieces
    first_oth += [swap(after(piece, attended[2][3])) for piece in first_pieces[1:]]
    down_oth = [swap(after(piece, attended[2][3])) for piece in down_pieces]
    ctx_parts = [one[0] for one in attended]
    ctx_oth = swap(jnp.concatenate([one[1] for one in attended], axis=1))
    up_parts = b_up.reshape(2, hidden)
    up_bias = jnp.where(side == 0, up_parts, up_parts[::-1])
    vectors = jnp.stack([b_out, gain_one, shift_one, b_down, gain_two, shift_two])
    output, dz, dctx_own, dctx_oth, sums, sent_f, kept_f, sent_d, kept_d = middle(
        blocks,
        ctx_parts,
        ctx_oth,
        layer_in,
        cotangent,
        vectors,
        up_bias,
        [first_pieces, first_oth, down_pieces, down_oth],
    )
    d_ctx_b = swap(dctx_oth)
    scatter_down = Scatter([kept_d, swap(sent_d)], added=True)
    scatter_first = Scatter([kept_f, swap(sent_f)], added=True)

    up_rows = hidden // width
    sent_sums = jnp.concatenate([sums[:6], sums[6 + up_rows :]], axis=0)
    both_sums = sums[: 6 + up_rows] + swap(sent_sums)

    def back(group, first, last, *others):
        ctx_t, lse = attended[group][2:]
        return attend_back(
            first, last, after(q_t, *others), keyed, valued, ctx_t, lse, dctx_own, d_ctx_b, extra
        )

    backs = [back(0, 0, 1)]
    scatter_down.step(backs[0][3])
    first_3 = scatter_first.step(backs[0][3])
    backs.append(back(1, 1, 2, backs[0][3]))
    backs.append(back(2, 2, 3, backs[1][3]))
    scatter_down.step(backs[2][3])
    d_parts = [one[:3] for one in backs]
    qkv_kept = grad_qkv_pieces(blocks, x_t, d_parts)
    scatter_qkv = Scatter(qkv_kept)
    qkv_3 = scatter_qkv.step()
    kept, sent = input_grad(blocks, d_parts, after(dz, qkv_kept[0]), gather_qkv.pieces)
    qv = jnp.concatenate([one[3][:2] for one in backs], axis=1).reshape(1, 2 * half)
    sum_all = Sum(jnp.concatenate([both_sums, qv], axis=0))
    scatter_first.step(kept)
    down_1 = scatter_down.step(kept)
    oth_dx = swap(sent)
    sum_all.step(kept)
    qkv_2 = scatter_qkv.step(kept)
    scatter_down.step(qkv_3)
    first_1 = scatter_first.step(qkv_3)
    sum_all.step(qkv_3)
    grad_input = (kept + oth_dx.astype(F32)).astype(BF16)
    qkv_1 = scatter_qkv.step(down_1)
    sum_all.step(qkv_2)
    scatter_first.step(qkv_2)
    scatter_qkv.step(first_1)
    sum_all.step(qkv_1)
    totals = sum_all.value
    grad_qkv = scatter_qkv.result().reshape(shard_rows, half // PAIR, 3, PAIR).transpose(0, 2, 1, 3)
    grad_first, grad_down = scatter_first.result(), scatter_down.result()

    return (
        output,
        grad_input,
        grad_qkv.reshape(shard_rows, 3, half),
        totals[6 + up_rows].reshape(2, half),
        grad_first[:, :half],
        totals[0],
        totals[1],
        totals[2],
        grad_first[:, half:],
        totals[6 : 6 + up_rows].reshape(hidden),
        grad_down,
        totals[3],
        totals[4],
        totals[5],
    )


def solution(mesh):
    placed = (
        P(("dp", "tensor"), None),
        P("dp"),
        P("dp", None, "tensor"),
        P(),
        P("dp", "tensor"),
        P(),
        P(),
        P(),
        P("dp", "tensor"),
        P(),
        P("dp", "tensor"),
        P(),
        P(),
        P(),
        P(("dp", "tensor"), None),
    )
    return jax.shard_map(
        per_device,
        mesh=mesh,
        in_specs=placed,
        out_specs=(
            P(("dp", "tensor"), None),
            P(("dp", "tensor"), None),
            P("dp", None, "tensor"),
            P(None, "tensor"),
            P("dp", "tensor"),
            P(),
            P(),
            P(),
            P("dp", "tensor"),
            P("tensor"),
            P("dp", "tensor"),
            P(),
            P(),
            P(),
        ),
        check_vma=False,
    )
```

```python
import functools
import math

import jax
import jax.numpy as jnp
from jax import lax
from jax.experimental import pallas as pl
from jax.experimental.pallas import tpu as pltpu
from jax.sharding import PartitionSpec as P

HEAD_DIM = 64
PAIR = 2 * HEAD_DIM
EPS = 1e-05
NEG = -1e30
F32 = jnp.float32
BF16 = jnp.bfloat16
VMEM_LIMIT = 60 << 20


def dot(left, right, left_dim=1, right_dim=0):
    return lax.dot_general(
        left, right, (((left_dim,), (right_dim,)), ((), ())), preferred_element_type=F32
    )


def params(**more):
    return pltpu.CompilerParams(vmem_limit_bytes=VMEM_LIMIT, **more)


def cost(flops, size, trans=0):
    return pl.CostEstimate(
        flops=int(flops) // 10, bytes_accessed=int(size) // 10, transcendentals=int(trans) // 10
    )


WHOLE = pl.BlockSpec(memory_space=pltpu.VMEM)
SCALARS = pl.BlockSpec(memory_space=pltpu.SMEM)
LEFT = pl.BlockSpec(memory_space=pl.ANY)


def swap(value):
    return lax.ppermute(value, "tensor", [(0, 1), (1, 0)])


def by_hops():
    return lax.axis_size("dp") == 16


ORDERS = ((8, 4, 1, 2), (2, 8, 4, 1))


def offsets(core):
    found = [0]
    for step in ORDERS[core]:
        found += [one ^ step for one in found]
    return found


def hop(value, level):
    pairs = [
        (2 * device + core, 2 * (device ^ ORDERS[core][level]) + core)
        for device in range(16)
        for core in range(2)
    ]
    return lax.ppermute(value, ("dp", "tensor"), pairs)


def row_blocks(side):
    if not by_hops():
        return jnp.zeros((2, 1), jnp.int32)
    table = jnp.array([offsets(0), offsets(1)], jnp.int32)
    return lax.axis_index("dp").astype(jnp.int32) ^ jnp.where(side == 0, table, table[::-1])


def after(value, *others):
    return lax.optimization_barrier((value, others))[0] if others else value


class Gather:
    def __init__(self, shard):
        self.held = shard[None]
        self.level = 0

    def step(self, *others):
        held = self.sent = after(self.held, *others)
        if not by_hops():
            if self.level == 0:
                self.pieces = [lax.all_gather(held[0], "dp", axis=0, tiled=True)[None]]
            self.level += 1
            return self.pieces[0]
        got = hop(held, self.level)
        self.level += 1
        if self.level < 4:
            self.held = jnp.concatenate([held, got], axis=0)
        self.pieces = [held, got]
        return got


class Scatter:
    def __init__(self, pieces, added=False):
        self.parts = list(pieces)
        self.level = 4
        self.added = added

    def total(self, at):
        return functools.reduce(lambda a, b: a + b, [part[at].astype(F32) for part in self.parts])

    def step(self, *others):
        self.level -= 1
        if not by_hops():
            if self.level == 3:
                whole = after(self.parts[0][0], *others).astype(F32)
                if self.added:
                    whole = whole + self.parts[1][0].astype(F32)
                self.sums = lax.psum_scatter(whole, "dp", scatter_dimension=0, tiled=True)
            self.sent = self.sums
            return self.sums
        if self.level == 3 and not self.added:
            self.parts, sent = self.parts[:1], self.parts[1]
        else:
            size = 1 << self.level
            sent = self.total(slice(size, 2 * size)).astype(BF16)
        self.sent = after(sent, *others)
        got = hop(self.sent, self.level)
        self.parts.append(got)
        return got

    def result(self):
        return self.total(0) if by_hops() else self.sums


class Sum:
    def __init__(self, value):
        self.value = value
        self.level = 0

    def step(self, *others):
        value = after(self.value, *others)
        if by_hops():
            step = ORDERS[0][self.level]
            value = value + lax.ppermute(value, "dp", [(i, i ^ step) for i in range(16)])
        elif self.level == 0:
            value = lax.psum(value, "dp")
        self.value = value
        self.level += 1
        return value


class Mover:
    def __init__(self, sems):
        self.sems = sems
        self.count = 0

    def copy(self, source, target):
        made = pltpu.make_async_copy(source, target, self.sems.at[self.count])
        self.count += 1
        return made

    def start(self, source, target):
        made = self.copy(source, target)
        made.start()
        return made


def wait(copies):
    for copy in copies:
        copy.wait()


def load_weight(mover, blocks, side, pieces, whole, start=0, size=None):
    copies = []
    size = whole.shape[1] if size is None else size
    columns = pl.ds(start, size)
    for piece in pieces:
        rows = piece.shape[1]
        for sub in range(piece.shape[0]):
            at = pl.multiple_of(blocks[side, len(copies)] * rows, 16)
            copies.append(
                mover.copy(piece.at[sub, :, columns], whole.at[pl.ds(at, rows), columns])
            )
    return copies


def store_pieces(blocks, outs, column, tile, side=0):
    place = 0
    for out in outs:
        rows = out.shape[1]
        for sub in range(out.shape[0]):
            at = pl.multiple_of(blocks[side, place] * rows, 16)
            out[sub, :, column : column + tile.shape[1]] = tile[pl.ds(at, rows), :]
            place += 1


def piece_shapes(blocks, rows, columns):
    if blocks == 1:
        return [jax.ShapeDtypeStruct((1, rows, columns), BF16)]
    return [jax.ShapeDtypeStruct((blocks // 2, rows // blocks, columns), BF16)] * 2


def head_rows(shape, head):
    row = lax.broadcasted_iota(jnp.int32, shape, 0)
    return (row >= head * HEAD_DIM) & (row < (head + 1) * HEAD_DIM)


def project_kernel(count, blocks, own, oth, bias, *rest):
    pieces = rest[:count]
    q_out, k_out, v_out, weight, sems = rest[count:]
    half = weight.shape[1] // 3
    rows = own.shape[0]
    copies = load_weight(Mover(sems), blocks, 0, pieces, weight)
    for copy in copies:
        copy.start()
    wait(copies)
    for place, ref in enumerate((own, oth)):
        lines = slice(place * rows, (place + 1) * rows)
        proj = (dot(ref[...], weight[...]) + bias[...]).astype(BF16)
        for at in range(0, half, PAIR):
            q_out[at : at + PAIR, lines] = (
                (proj[:, at : at + PAIR].astype(F32) * HEAD_DIM**-0.5).T.astype(BF16)
            )
        k_out[lines, :] = proj[:, half : 2 * half]
        v_out[lines, :] = proj[:, 2 * half :]


def project(blocks, own, oth, bias, pieces):
    rows, width = own.shape
    seq = 2 * rows
    columns = bias.shape[1]
    half = columns // 3
    shape = jax.ShapeDtypeStruct
    return pl.pallas_call(
        functools.partial(project_kernel, len(pieces)),
        in_specs=[SCALARS, WHOLE, WHOLE, WHOLE] + [LEFT] * len(pieces),
        out_specs=[WHOLE] * 3,
        out_shape=[shape((half, seq), BF16), shape((seq, half), BF16), shape((seq, half), BF16)],
        scratch_shapes=[pltpu.VMEM((width, columns), BF16), pltpu.SemaphoreType.DMA((16,))],
        compiler_params=params(),
        cost_estimate=cost(2 * seq * width * columns, 6 << 20),
        name="project",
    )(blocks, own, oth, bias, *pieces)


def attend_kernel(q_ref, k_ref, v_ref, extra, ctx_a, ctx_b, ctx_t, lse_out):
    rows = ctx_a.shape[0]
    seq = k_ref.shape[0]
    q_t = q_ref[...].astype(F32)
    v_t = v_ref[...].astype(F32).T
    k_aug = jnp.concatenate([k_ref[...], extra[...]], axis=1)
    tail_row = lax.broadcasted_iota(jnp.int32, (PAIR, seq), 0)
    tail = jnp.where(tail_row == 3, 1.0, 0.0).astype(BF16)
    step = min(256, seq)
    q_augs, v_augs = [], []
    for head in range(2):
        mine = head_rows((PAIR, seq), head)
        q_augs.append(
            jnp.concatenate([jnp.where(mine, q_t, 0.0).astype(BF16), tail], axis=0)
        )
        v_augs.append(jnp.where(mine, v_t, 1.0).astype(BF16))
    work = [(head, at) for head in range(2) for at in range(0, seq, step)]

    def scores_of(head, at):
        return dot(k_aug, q_augs[head][:, at : at + step])

    following = scores_of(*work[0])
    for place, (head, at) in enumerate(work):
        scores = following
        if place + 1 < len(work):
            following = scores_of(*work[place + 1])
        top = jnp.max(scores, axis=0, keepdims=True)
        expo = jnp.exp(scores - top).astype(BF16)
        both = dot(v_augs[head], expo)
        own_at, oth_at = head * HEAD_DIM, (1 - head) * HEAD_DIM
        total = both[oth_at : oth_at + HEAD_DIM]
        ctx_t[own_at : own_at + HEAD_DIM, at : at + step] = (
            both[own_at : own_at + HEAD_DIM] / total
        ).astype(BF16)
        lse_out[head : head + 1, at : at + step] = top + jnp.log(total[0:1])
    turned = ctx_t[...].astype(F32).T.astype(BF16)
    ctx_a[...] = turned[:rows]
    ctx_b[...] = turned[rows:]


def pair_specs(first, seq):
    wide = pl.BlockSpec((PAIR, seq), lambda i: (first + i, 0))
    tall = pl.BlockSpec((seq, PAIR), lambda i: (0, first + i))
    tall_half = pl.BlockSpec((seq // 2, PAIR), lambda i: (0, first + i))
    return wide, tall, tall_half


def attend(first, last, q_t, keyed, valued, extra):
    seq = keyed.shape[0]
    count = last - first
    wide, tall, _ = pair_specs(first, seq)
    own_wide, _, own_half = pair_specs(0, seq)
    shape = jax.ShapeDtypeStruct
    return pl.pallas_call(
        attend_kernel,
        grid=(count,),
        in_specs=[wide, tall, tall, WHOLE],
        out_specs=[own_half, own_half, own_wide, pl.BlockSpec((8, seq), lambda i: (i, 0))],
        out_shape=[
            shape((seq // 2, count * PAIR), BF16),
            shape((seq // 2, count * PAIR), BF16),
            shape((count * PAIR, seq), BF16),
            shape((count * 8, seq), F32),
        ],
        compiler_params=params(),
        cost_estimate=cost(64 * count * seq * seq * PAIR, 2 << 20, count * seq * seq * 2),
        name="attend",
    )(q_t, keyed, valued, extra)


def three_parts(value):
    high = value.astype(BF16).astype(F32)
    mid = (value - high).astype(BF16).astype(F32)
    return high, mid, value - high - mid


def attend_back_kernel(q_t, keyed, valued, ctx_t, lse, d_a, d_b, extra, dq, dk, dv, sums, d_qt):
    seq = keyed.shape[0]
    tail_row = lax.broadcasted_iota(jnp.int32, (PAIR, seq), 0)

    def tail(parts, mask):
        rows = jnp.where(tail_row == 3, mask, 0.0)
        for place, part in enumerate(parts):
            rows = jnp.where(tail_row == place, part, rows)
        return rows.astype(BF16)

    d_t = jnp.concatenate([d_a[...].astype(F32).T, d_b[...].astype(F32).T], axis=1)
    q_full = q_t[...].astype(F32)
    product = d_t * ctx_t[...].astype(F32)
    k_aug = jnp.concatenate([keyed[...], extra[...]], axis=1)
    v_aug = jnp.concatenate([valued[...], extra[...]], axis=1)
    k_t = keyed[...].astype(F32).T.astype(BF16)
    step = min(256, seq)
    q_heads, d_heads, q_augs, d_augs = [], [], [], []
    for head in range(2):
        mine = head_rows((PAIR, seq), head)
        delta = jnp.sum(
            product[head * HEAD_DIM : (head + 1) * HEAD_DIM], axis=0, keepdims=True
        )
        q_heads.append(jnp.where(mine, q_full, 0.0).astype(BF16))
        d_heads.append(jnp.where(mine, d_t, 0.0).astype(BF16))
        q_augs.append(
            jnp.concatenate([q_heads[head], tail(three_parts(-lse[head : head + 1, :]), 1.0)], axis=0)
        )
        d_augs.append(jnp.concatenate([d_heads[head], tail(three_parts(-delta), 0.0)], axis=0))
    work = [(at, head) for at in range(0, seq, step) for head in range(2)]

    def products(at, head):
        keys = slice(at, at + step)
        return dot(k_aug[keys], q_augs[head]), dot(v_aug[keys], d_augs[head])

    following = products(*work[0])
    key_sum = value_sum = None
    for place, (at, head) in enumerate(work):
        keys = slice(at, at + step)
        scores, d_probs = following
        if place + 1 < len(work):
            following = products(*work[place + 1])
        probs = jnp.exp(scores)
        d_scores = (probs * d_probs).astype(BF16)
        part = dot(probs.astype(BF16), d_heads[head], 1, 1)
        value_sum = part if head == 0 else value_sum + part
        part = dot(d_scores, q_heads[head], 1, 1)
        key_sum = part if head == 0 else key_sum + part
        lines = slice(head * HEAD_DIM, (head + 1) * HEAD_DIM)
        part = dot(k_t[lines, keys], d_scores)
        if at == 0:
            d_qt[lines, :] = part
        else:
            d_qt[lines, :] += part
        if head == 1:
            dk[keys, :] = key_sum.astype(BF16)
            dv[keys, :] = value_sum.astype(BF16)
    dq[...] = (d_qt[...] * HEAD_DIM**-0.5).T.astype(BF16)
    sums[...] = jnp.zeros(sums.shape, F32)
    sums[0:1, :] = jnp.sum(dq[...].astype(F32), axis=0, keepdims=True)
    sums[1:2, :] = jnp.sum(dv[...].astype(F32), axis=0, keepdims=True)


def attend_back(first, last, q_t, keyed, valued, ctx_t, lse, d_a, d_b, extra):
    seq = keyed.shape[0]
    count = last - first
    wide, tall, tall_half = pair_specs(first, seq)
    own_wide, own_tall, _ = pair_specs(0, seq)
    shape = jax.ShapeDtypeStruct
    return pl.pallas_call(
        attend_back_kernel,
        grid=(count,),
        in_specs=[
            wide,
            tall,
            tall,
            own_wide,
            pl.BlockSpec((8, seq), lambda i: (i, 0)),
            tall_half,
            tall_half,
            WHOLE,
        ],
        out_specs=[own_tall] * 3 + [pl.BlockSpec((8, PAIR), lambda i: (0, i))],
        out_shape=[shape((seq, count * PAIR), BF16)] * 3 + [shape((8, count * PAIR), F32)],
        scratch_shapes=[pltpu.VMEM((PAIR, seq), F32)],
        compiler_params=params(),
        cost_estimate=cost(64 * count * seq * seq * PAIR, 3 << 20, count * seq * seq * 2),
        name="attend_back",
    )(q_t, keyed, valued, ctx_t, lse, d_a, d_b, extra)


def row_mean(value):
    return jnp.mean(value, axis=1, keepdims=True)


def normed(value):
    centred = value - row_mean(value)
    rate = lax.rsqrt(row_mean(centred * centred) + EPS)
    return centred * rate, rate


def norm_back(grad, hat, rate, gain):
    scaled = grad * gain
    return rate * (scaled - row_mean(scaled) - hat * row_mean(scaled * hat))


def column_sum(value):
    return jnp.sum(value, axis=0, keepdims=True)


def gelu(value):
    phi = 0.5 + 0.5 * lax.erf(value * (0.5**0.5))
    return phi, jnp.exp(value * value * -0.5) * (1.0 / math.sqrt(2.0 * math.pi))


def hidden_spans(hidden, chunk):
    return [(side, at, side * hidden + at) for side in range(2) for at in range(0, hidden, chunk)]


CHUNK = 512


def middle_kernel(count, parts, blocks, *rest):
    ctx_parts = rest[:parts]
    ctx_oth, x_ref, cot_ref, vectors, b_up = rest[parts : parts + 5]
    rest = rest[parts + 5 :]
    pieces = [rest[at : at + count] for at in range(0, 4 * count, count)]
    rest = rest[4 * count :]
    out, dz, dctx_own, dctx_oth, sums, sent_f, kept_f, sent_d, kept_d = rest[:9]
    w_own, w_oth, down_own, down_oth = rest[9:13]
    ctx_s, x_s, cot_s, act_s, slope_s, y_t, d_t, dz_t = rest[13:21]
    out_s, dz_s, dctx_s, tile, got_f, got_d, sems = rest[21:]
    wholes, downs = (w_own, w_oth), (down_own, down_oth)
    half = ctx_oth.shape[1]
    hidden = down_own.shape[1]
    width = x_ref.shape[1]
    mover = Mover(sems)
    stores = []

    inputs, at = [], 0
    for part in ctx_parts:
        size = part.shape[1]
        inputs.append(mover.start(part, ctx_s.at[0, :, pl.ds(at, size)]))
        at += size
    inputs.append(mover.start(ctx_oth, ctx_s.at[1]))
    loads = []
    for span in ((0, half), (half, hidden)):
        for side in range(2):
            loads.append(load_weight(mover, blocks, side, pieces[side], wholes[side], *span))
    for side in range(2):
        loads.append(load_weight(mover, blocks, side, pieces[2 + side], downs[side]))
    for place, load in enumerate(loads):
        for copy in load:
            copy.start()
        if place == 1:
            inputs.append(mover.start(x_ref, x_s))
    late = mover.start(cot_ref, cot_s)
    wait(inputs + loads[0] + loads[1])

    def put(tiles, lefts, rights, side, held, out_ref):
        for left, right, at, size, column in tiles:
            tile[:, :size] = dot(lefts[left][...], rights[right][:, at : at + size]).astype(BF16)
            store_pieces(blocks, [held], column, tile.at[:, pl.ds(0, size)], side)
            span = pl.ds(column, size)
            stores.append(mover.start(held.at[:, :, span], out_ref.at[:, :, span]))

    b_out, gain_one, shift_one = vectors[0:1, :], vectors[1:2, :], vectors[2:3, :]
    b_down, gain_two, shift_two = vectors[3:4, :], vectors[4:5, :], vectors[5:6, :]
    attn = dot(ctx_s[0], w_own[:, :half], 1, 1) + dot(ctx_s[1], w_oth[:, :half], 1, 1)
    hat_one, rate_one = normed(attn + b_out + x_s[...].astype(F32))
    y_one = hat_one * gain_one + shift_one
    low = y_one.astype(BF16)
    spans = hidden_spans(hidden, CHUNK)
    ffn = None
    wait(loads[2] + loads[3])

    def pre_of(side, at, _):
        pre = dot(low, wholes[side][:, half + at : half + at + CHUNK])
        return pre + b_up[side : side + 1, at : at + CHUNK]

    following = pre_of(*spans[0])
    for number, (side, at, place) in enumerate(spans):
        pre = following
        if number + 1 < len(spans):
            following = pre_of(*spans[number + 1])
        phi, bell = gelu(pre)
        act = (pre * phi).astype(BF16)
        act_s[:, place : place + CHUNK] = act
        slope_s[:, place : place + CHUNK] = (phi + pre * bell).astype(BF16)
        if number == 0:
            wait(loads[4] + loads[5])
        part = dot(act, downs[side][:, at : at + CHUNK], 1, 1)
        ffn = part if ffn is None else ffn + part
    hat_two, rate_two = normed(ffn + b_down + y_one)
    out_s[...] = (hat_two * gain_two + shift_two).astype(BF16)
    stores.append(mover.start(out_s, out))
    late.wait()
    cot = cot_s[...].astype(F32)
    d_two = norm_back(cot, hat_two, rate_two, gain_two)
    d_ffn = d_two.astype(BF16)
    d_t[...] = d_two.T.astype(BF16)
    y_t[...] = y_one.T.astype(BF16)
    sums[3:4, :] = column_sum(d_two)
    sums[4:5, :] = column_sum(cot * hat_two)
    sums[5:6, :] = column_sum(cot)
    for side, (held, out_ref) in ((1, (got_d.at[1], sent_d)), (0, (got_d.at[0], kept_d))):
        tiles = [(0, 0, side * hidden + at, CHUNK, at) for at in range(0, hidden, CHUNK)]
        put(tiles, [d_t], [act_s], side, held, out_ref)
    back = None

    def d_act_of(side, at, _):
        return dot(d_ffn, downs[side][:, at : at + CHUNK])

    following = d_act_of(*spans[0])
    for number, (side, at, place) in enumerate(spans):
        d_act = following
        if number + 1 < len(spans):
            following = d_act_of(*spans[number + 1])
        d_pre = (d_act * slope_s[:, place : place + CHUNK].astype(F32)).astype(BF16)
        slope_s[:, place : place + CHUNK] = d_pre
        total = column_sum(d_pre.astype(F32))
        for col in range(0, CHUNK, 256):
            spot = place + col
            row, left = 6 + spot // width, spot % width
            sums[row : row + 1, left : left + 256] = total[:, col : col + 256]
        part = dot(d_pre, wholes[side][:, half + at : half + at + CHUNK], 1, 1)
        back = part if back is None else back + part
    d_one = d_two + back
    d_zero = norm_back(d_one, hat_one, rate_one, gain_one)
    dz_s[...] = d_zero
    stores.append(mover.start(dz_s, dz))
    d_attn = d_zero.astype(BF16)
    dctx_s[0] = dot(d_attn, w_own[:, :half]).astype(BF16)
    dctx_s[1] = dot(d_attn, w_oth[:, :half]).astype(BF16)
    stores.append(mover.start(dctx_s.at[0], dctx_own))
    stores.append(mover.start(dctx_s.at[1], dctx_oth))
    dz_t[...] = d_zero.T.astype(BF16)
    sums[0:1, :] = column_sum(d_zero)
    sums[1:2, :] = column_sum(d_one * hat_one)
    sums[2:3, :] = column_sum(d_one)
    for side, (held, out_ref) in ((1, (got_f.at[1], sent_f)), (0, (got_f.at[0], kept_f))):
        tiles = [
            (1, 1, side * hidden + at, CHUNK, half + at) for at in range(0, hidden, CHUNK)
        ] + [(0, 0, 0, half, 0)]
        put(tiles, [dz_t, y_t], [ctx_s.at[side], slope_s], side, held, out_ref)
    wait(stores)


def middle(blocks, ctx_parts, ctx_oth, own, cotangent, vectors, b_up, pieces):
    rows, width = own.shape
    half = ctx_oth.shape[1]
    hidden = b_up.shape[1]
    shape = jax.ShapeDtypeStruct
    count = len(pieces[0])
    sum_rows = 6 + 2 * hidden // width
    flops = 2 * rows * width * (6 * half + 12 * hidden)
    number = blocks.shape[1]
    first = (number, width // number, half + hidden)
    down = (number, width // number, hidden)
    vmem = pltpu.VMEM
    return pl.pallas_call(
        functools.partial(middle_kernel, count, len(ctx_parts)),
        in_specs=[SCALARS]
        + [LEFT] * (len(ctx_parts) + 3)
        + [WHOLE, WHOLE]
        + [LEFT] * (4 * count),
        out_specs=[LEFT] * 4 + [WHOLE] + [LEFT] * 4,
        out_shape=[
            shape((rows, width), BF16),
            shape((rows, width), F32),
            shape((rows, half), BF16),
            shape((rows, half), BF16),
            shape((sum_rows, width), F32),
            shape(first, BF16),
            shape(first, BF16),
            shape(down, BF16),
            shape(down, BF16),
        ],
        scratch_shapes=[vmem((width, half + hidden), BF16)] * 2
        + [vmem((width, hidden), BF16)] * 2
        + [
            vmem((2, rows, half), BF16),
            vmem((rows, width), BF16),
            vmem((rows, width), BF16),
            vmem((rows, 2 * hidden), BF16),
            vmem((rows, 2 * hidden), BF16),
            vmem((width, rows), BF16),
            vmem((width, rows), BF16),
            vmem((width, rows), BF16),
            vmem((rows, width), BF16),
            vmem((rows, width), F32),
            vmem((2, rows, half), BF16),
            vmem((width, CHUNK), BF16),
            vmem((2, *first), BF16),
            vmem((2, *down), BF16),
            pltpu.SemaphoreType.DMA((144,)),
        ],
        compiler_params=params(),
        cost_estimate=cost(flops, 28 << 20, rows * hidden * 4),
        name="middle",
    )(
        blocks,
        *ctx_parts,
        ctx_oth,
        own,
        cotangent,
        vectors,
        b_up,
        *[piece for group in pieces for piece in group],
    )


def pair_places(parts):
    return [
        (group, at) for group, part in enumerate(parts) for at in range(0, part[0].shape[1], PAIR)
    ]


def grad_qkv_kernel(groups, blocks, x_t, *refs):
    parts = [refs[3 * group : 3 * group + 3] for group in range(groups)]
    refs = refs[3 * groups :]
    x_s, right_s, tile, sems = refs[-4:]
    outs, held = refs[:-6], refs[-6:-4]
    held = held[: len(outs)]
    mover = Mover(sems)
    loads = [mover.start(x_t, x_s)]
    places = pair_places(parts)
    for pair, (group, at) in enumerate(places):
        loads.append(
            [
                mover.start(
                    part.at[:, pl.ds(at, PAIR)], right_s.at[pair, :, pl.ds(kind * PAIR, PAIR)]
                )
                for kind, part in enumerate(parts[group])
            ]
        )
    loads[0].wait()
    stores = []
    for pair in range(len(places)):
        wait(loads[1 + pair])
        tile[...] = dot(x_s[...], right_s[pair]).astype(BF16)
        column = 3 * PAIR * pair
        store_pieces(blocks, held, column, tile)
        span = pl.ds(column, 3 * PAIR)
        for mine, out in zip(held, outs):
            stores.append(mover.start(mine.at[:, :, span], out.at[:, :, span]))
    wait(stores)


def grad_qkv_pieces(blocks, x_t, d_parts):
    width, seq = x_t.shape
    flat = [part for parts in d_parts for part in parts]
    columns = sum(part.shape[1] for part in flat)
    shapes = piece_shapes(blocks.shape[1], width, columns)
    held = [pltpu.VMEM(one.shape, BF16) for one in shapes]
    held += [pltpu.VMEM((8, 128), BF16)] * (2 - len(held))
    return pl.pallas_call(
        functools.partial(grad_qkv_kernel, len(d_parts)),
        in_specs=[SCALARS] + [LEFT] * (1 + len(flat)),
        out_specs=[LEFT] * len(shapes),
        out_shape=shapes,
        scratch_shapes=held
        + [
            pltpu.VMEM((width, seq), BF16),
            pltpu.VMEM((columns // (3 * PAIR), seq, 3 * PAIR), BF16),
            pltpu.VMEM((width, 3 * PAIR), BF16),
            pltpu.SemaphoreType.DMA((32,)),
        ],
        compiler_params=params(),
        cost_estimate=cost(2 * seq * width * columns, 6 << 20),
        name="grad_qkv",
    )(blocks, x_t, *flat)


def input_kernel(count, groups, blocks, *refs):
    parts = [refs[3 * group : 3 * group + 3] for group in range(groups)]
    refs = refs[3 * groups :]
    dz, pieces = refs[0], refs[1 : 1 + count]
    kept, sent, weight, whole, dz_s, sent_s, sems = refs[1 + count :]
    mover = Mover(sems)
    rows = kept.shape[0]
    half = whole.shape[1] // 3
    loads = load_weight(mover, blocks, 0, pieces, weight)
    for pair, (group, at) in enumerate(pair_places(parts)):
        for kind, part in enumerate(parts[group]):
            target = whole.at[:, pl.ds(kind * half + pair * PAIR, PAIR)]
            loads.append(mover.copy(part.at[:, pl.ds(at, PAIR)], target))
    for copy in loads:
        copy.start()
    last = mover.start(dz, dz_s)
    wait(loads)
    sent_s[...] = dot(whole[rows:, :], weight[...], 1, 1).astype(BF16)
    store = mover.start(sent_s, sent)
    last.wait()
    dz_s[...] += dot(whole[:rows, :], weight[...], 1, 1)
    mover.start(dz_s, kept).wait()
    store.wait()


def input_grad(blocks, d_parts, dz, pieces):
    rows, width = dz.shape
    flat = [part for parts in d_parts for part in parts]
    columns = sum(part.shape[1] for part in flat)
    shape = jax.ShapeDtypeStruct
    return pl.pallas_call(
        functools.partial(input_kernel, len(pieces), len(d_parts)),
        in_specs=[SCALARS] + [LEFT] * (len(flat) + 1 + len(pieces)),
        out_specs=[LEFT] * 2,
        out_shape=[shape((rows, width), F32), shape((rows, width), BF16)],
        scratch_shapes=[
            pltpu.VMEM((width, columns), BF16),
            pltpu.VMEM((2 * rows, columns), BF16),
            pltpu.VMEM((rows, width), F32),
            pltpu.VMEM((rows, width), BF16),
            pltpu.SemaphoreType.DMA((48,)),
        ],
        compiler_params=params(),
        cost_estimate=cost(4 * rows * width * columns, 8 << 20),
        name="input_grad",
    )(blocks, *flat, dz, *pieces)


def per_device(
    layer_in,
    seq_lens,
    w_qkv,
    b_qv,
    w_out,
    b_out,
    gain_one,
    shift_one,
    w_up,
    b_up,
    w_down,
    b_down,
    gain_two,
    shift_two,
    cotangent,
):
    rows, width = layer_in.shape
    seq = 2 * rows
    side = lax.axis_index("tensor")
    shard_rows, _, half = w_qkv.shape
    hidden = w_up.shape[1]
    blocks = row_blocks(side)
    pairs = range(half // PAIR)

    gather_qkv = Gather(w_qkv.reshape(shard_rows, 3 * half))
    gather_first = Gather(jnp.concatenate([w_out, w_up], axis=1))
    gather_down = Gather(w_down)
    oth_in = swap(layer_in)
    qkv_0 = gather_qkv.step()
    gather_first.step(qkv_0)
    qkv_1 = gather_qkv.step()
    gather_first.step(qkv_1)
    qkv_2 = gather_qkv.step()
    gather_down.step(qkv_2)
    qkv_3 = gather_qkv.step()
    gather_first.step(qkv_3)
    x_t = jnp.concatenate([after(layer_in, qkv_0), oth_in], axis=0).T

    bias_qv = lax.dynamic_slice_in_dim(b_qv, side * half, half, 1)
    bias = jnp.concatenate([bias_qv[0:1], jnp.zeros((1, half), F32), bias_qv[1:2]], axis=1)
    row = jnp.arange(seq, dtype=jnp.int32)
    position = ((row // rows) ^ side) * rows + row % rows
    lane = jnp.arange(PAIR, dtype=jnp.int32)[None, :]
    masked = jnp.where(position < seq_lens[0], 0.0, NEG)[:, None]
    extra = jnp.where(lane < 3, 1.0, jnp.where(lane == 3, masked, 0.0)).astype(BF16)

    q_t, keyed, valued = project(blocks, layer_in, oth_in, bias, gather_qkv.pieces)
    gather_down.step(qkv_3)
    gather_first.step()
    gather_down.step(q_t)
    first_pieces, down_pieces = gather_first.pieces, gather_down.pieces
    attended = [
        attend(0, 1, after(q_t, gather_first.sent), keyed, valued, extra)
    ]
    gather_down.step(attended[0][3])
    down_pieces = gather_down.pieces
    first_oth = [swap(after(first_pieces[0], attended[0][3]))]
    attended.append(
        attend(1, 2, after(q_t, attended[0][3], gather_down.sent), keyed, valued, extra)
    )
    first_oth += [swap(after(piece, attended[1][3])) for piece in first_pieces[1:]]
    down_oth = [swap(after(down_pieces[0], attended[1][3]))]
    attended.append(attend(2, 3, after(q_t, attended[1][3]), keyed, valued, extra))
    down_oth += [swap(after(piece, attended[2][3])) for piece in down_pieces[1:]]
    ctx_parts = [one[0] for one in attended]
    ctx_oth = swap(jnp.concatenate([one[1] for one in attended], axis=1))
    up_parts = b_up.reshape(2, hidden)
    up_bias = jnp.where(side == 0, up_parts, up_parts[::-1])
    vectors = jnp.stack([b_out, gain_one, shift_one, b_down, gain_two, shift_two])
    output, dz, dctx_own, dctx_oth, sums, sent_f, kept_f, sent_d, kept_d = middle(
        blocks,
        ctx_parts,
        ctx_oth,
        layer_in,
        cotangent,
        vectors,
        up_bias,
        [first_pieces, first_oth, down_pieces, down_oth],
    )
    d_ctx_b = swap(dctx_oth)
    scatter_down = Scatter([kept_d, swap(sent_d)], added=True)
    scatter_first = Scatter([kept_f, swap(sent_f)], added=True)

    up_rows = hidden // width
    sent_sums = jnp.concatenate([sums[:6], sums[6 + up_rows :]], axis=0)
    both_sums = sums[: 6 + up_rows] + swap(sent_sums)

    def back(group, first, last, *others):
        ctx_t, lse = attended[group][2:]
        return attend_back(
            first, last, after(q_t, *others), keyed, valued, ctx_t, lse, dctx_own, d_ctx_b, extra
        )

    backs = [back(0, 0, 1)]
    scatter_down.step(backs[0][3])
    first_3 = scatter_first.step(backs[0][3])
    backs.append(back(1, 1, 2, backs[0][3], scatter_down.sent, scatter_first.sent))
    scatter_down.step(backs[1][3])
    backs.append(back(2, 2, 3, backs[1][3], scatter_down.sent))
    d_parts = [one[:3] for one in backs]
    qkv_kept = grad_qkv_pieces(blocks, x_t, d_parts)
    scatter_qkv = Scatter(qkv_kept)
    qkv_3 = scatter_qkv.step()
    kept, sent = input_grad(
        blocks, d_parts, after(dz, qkv_kept[0], first_3), gather_qkv.pieces
    )
    qv = jnp.concatenate([one[3][:2] for one in backs], axis=1).reshape(1, 2 * half)
    sum_all = Sum(jnp.concatenate([both_sums, qv], axis=0))
    scatter_first.step(kept)
    down_1 = scatter_down.step(kept)
    oth_dx = swap(sent)
    sum_all.step(kept)
    qkv_2 = scatter_qkv.step(kept)
    scatter_down.step(qkv_3)
    first_1 = scatter_first.step(qkv_3)
    sum_all.step(qkv_3)
    grad_input = (kept + oth_dx.astype(F32)).astype(BF16)
    qkv_1 = scatter_qkv.step(down_1)
    sum_all.step(qkv_2)
    scatter_first.step(qkv_2)
    scatter_qkv.step(first_1)
    sum_all.step(qkv_1)
    totals = sum_all.value
    grad_qkv = scatter_qkv.result().reshape(shard_rows, half // PAIR, 3, PAIR).transpose(0, 2, 1, 3)
    grad_first, grad_down = scatter_first.result(), scatter_down.result()

    return (
        output,
        grad_input,
        grad_qkv.reshape(shard_rows, 3, half),
        totals[6 + up_rows].reshape(2, half),
        grad_first[:, :half],
        totals[0],
        totals[1],
        totals[2],
        grad_first[:, half:],
        totals[6 : 6 + up_rows].reshape(hidden),
        grad_down,
        totals[3],
        totals[4],
        totals[5],
    )


def solution(mesh):
    placed = (
        P(("dp", "tensor"), None),
        P("dp"),
        P("dp", None, "tensor"),
        P(),
        P("dp", "tensor"),
        P(),
        P(),
        P(),
        P("dp", "tensor"),
        P(),
        P("dp", "tensor"),
        P(),
        P(),
        P(),
        P(("dp", "tensor"), None),
    )
    return jax.shard_map(
        per_device,
        mesh=mesh,
        in_specs=placed,
        out_specs=(
            P(("dp", "tensor"), None),
            P(("dp", "tensor"), None),
            P("dp", None, "tensor"),
            P(None, "tensor"),
            P("dp", "tensor"),
            P(),
            P(),
            P(),
            P("dp", "tensor"),
            P("tensor"),
            P("dp", "tensor"),
            P(),
            P(),
            P(),
        ),
        check_vma=False,
    )
```

```python
import functools
import math

import jax
import jax.numpy as jnp
from jax import lax
from jax.experimental import pallas as pl
from jax.experimental.pallas import tpu as pltpu
from jax.sharding import PartitionSpec as P

HEAD_DIM = 64
PAIR = 2 * HEAD_DIM
EPS = 1e-05
NEG = -1e30
F32 = jnp.float32
BF16 = jnp.bfloat16
VMEM_LIMIT = 60 << 20


def dot(left, right, left_dim=1, right_dim=0):
    return lax.dot_general(
        left, right, (((left_dim,), (right_dim,)), ((), ())), preferred_element_type=F32
    )


def params(**more):
    return pltpu.CompilerParams(vmem_limit_bytes=VMEM_LIMIT, **more)


def cost(flops, size, trans=0):
    return pl.CostEstimate(
        flops=int(flops) // 10, bytes_accessed=int(size) // 10, transcendentals=int(trans) // 10
    )


WHOLE = pl.BlockSpec(memory_space=pltpu.VMEM)
SCALARS = pl.BlockSpec(memory_space=pltpu.SMEM)
LEFT = pl.BlockSpec(memory_space=pl.ANY)


def swap(value):
    return lax.ppermute(value, "tensor", [(0, 1), (1, 0)])


def by_hops():
    return lax.axis_size("dp") == 16


ORDERS = (((8, 4, 1, 2), (2, 8, 4, 1)), ((8, 4, 2, 1), (1, 8, 4, 2)))


def offsets(kind, core):
    found = [0]
    for step in ORDERS[kind][core]:
        found += [one ^ step for one in found]
    return found


def hop(value, level, kind):
    pairs = [
        (2 * device + core, 2 * (device ^ ORDERS[kind][core][level]) + core)
        for device in range(16)
        for core in range(2)
    ]
    return lax.ppermute(value, ("dp", "tensor"), pairs)


def row_blocks(side):
    if not by_hops():
        return jnp.zeros((4, 1), jnp.int32)
    tables = [
        jnp.array([offsets(kind, core) for kind in range(2) for core in order], jnp.int32)
        for order in ((0, 1), (1, 0))
    ]
    return lax.axis_index("dp").astype(jnp.int32) ^ jnp.where(side == 0, *tables)


def after(value, *others):
    return lax.optimization_barrier((value, others))[0] if others else value


class Gather:
    def __init__(self, shard, kind=0):
        self.held = shard[None]
        self.level = 0
        self.kind = kind

    def step(self, *others):
        held = self.sent = after(self.held, *others)
        if not by_hops():
            if self.level == 0:
                self.pieces = [lax.all_gather(held[0], "dp", axis=0, tiled=True)[None]]
            self.level += 1
            return self.pieces[0]
        got = hop(held, self.level, self.kind)
        self.level += 1
        if self.level < 4:
            self.held = jnp.concatenate([held, got], axis=0)
        self.pieces = [held, got]
        return got


class Scatter:
    def __init__(self, pieces, kind=0, added=False, extra=None):
        self.parts = list(pieces)
        self.kind = kind
        self.level = 4
        self.added = added
        self.extra = extra

    def extra_block(self, columns):
        high = lax.reduce_precision(self.extra, 8, 7)
        mid = lax.reduce_precision(self.extra - high, 8, 7)
        block = jnp.concatenate([high, mid, self.extra - high - mid], axis=0).astype(BF16)
        return jnp.pad(block, ((0, 0), (0, columns - block.shape[1])))[None]

    def add_extra(self, block):
        rows, width = self.extra.shape
        high, mid, low = [
            block[at : at + rows, :width].astype(F32) for at in range(0, 3 * rows, rows)
        ]
        self.extra = self.extra + ((high + mid) + low)

    def total(self, at):
        return functools.reduce(lambda a, b: a + b, [part[at].astype(F32) for part in self.parts])

    def step(self, *others):
        self.level -= 1
        if not by_hops():
            if self.level == 3:
                whole = after(self.parts[0][0], *others).astype(F32)
                if self.added:
                    whole = whole + self.parts[1][0].astype(F32)
                self.sums = lax.psum_scatter(whole, "dp", scatter_dimension=0, tiled=True)
                if self.extra is not None:
                    self.extra = lax.psum(self.extra, "dp")
            self.sent = self.sums
            return self.sums
        if self.level == 3 and not self.added:
            self.parts, sent = self.parts[:1], self.parts[1]
        else:
            size = 1 << self.level
            sent = self.total(slice(size, 2 * size)).astype(BF16)
        if self.extra is not None:
            sent = jnp.concatenate([sent, self.extra_block(sent.shape[2])], axis=0)
        self.sent = after(sent, *others)
        got = hop(self.sent, self.level, self.kind)
        if self.extra is not None:
            self.add_extra(got[-1])
        self.parts.append(got)
        return got

    def result(self):
        return self.total(0) if by_hops() else self.sums


class Mover:
    def __init__(self, sems):
        self.sems = sems
        self.count = 0

    def copy(self, source, target):
        made = pltpu.make_async_copy(source, target, self.sems.at[self.count])
        self.count += 1
        return made

    def start(self, source, target):
        made = self.copy(source, target)
        made.start()
        return made


def wait(copies):
    for copy in copies:
        copy.wait()


def load_weight(mover, blocks, side, pieces, whole, start=0, size=None):
    copies = []
    size = whole.shape[1] if size is None else size
    columns = pl.ds(start, size)
    for piece in pieces:
        rows = piece.shape[1]
        for sub in range(piece.shape[0]):
            at = pl.multiple_of(blocks[side, len(copies)] * rows, 16)
            copies.append(
                mover.copy(piece.at[sub, :, columns], whole.at[pl.ds(at, rows), columns])
            )
    return copies


def store_pieces(blocks, outs, column, tile, side=0):
    place = 0
    for out in outs:
        rows = out.shape[1]
        for sub in range(out.shape[0]):
            at = pl.multiple_of(blocks[side, place] * rows, 16)
            out[sub, :, column : column + tile.shape[1]] = tile[pl.ds(at, rows), :]
            place += 1


def piece_shapes(blocks, rows, columns):
    if blocks == 1:
        return [jax.ShapeDtypeStruct((1, rows, columns), BF16)]
    return [jax.ShapeDtypeStruct((blocks // 2, rows // blocks, columns), BF16)] * 2


def head_rows(shape, head):
    row = lax.broadcasted_iota(jnp.int32, shape, 0)
    return (row >= head * HEAD_DIM) & (row < (head + 1) * HEAD_DIM)


def project_kernel(count, blocks, own, oth, bias, *rest):
    pieces = rest[:count]
    q_out, k_out, v_out, weight, sems = rest[count:]
    half = weight.shape[1] // 3
    rows = own.shape[0]
    copies = load_weight(Mover(sems), blocks, 0, pieces, weight)
    for copy in copies:
        copy.start()
    wait(copies)
    for place, ref in enumerate((own, oth)):
        lines = slice(place * rows, (place + 1) * rows)
        proj = (dot(ref[...], weight[...]) + bias[...]).astype(BF16)
        for at in range(0, half, PAIR):
            q_out[at : at + PAIR, lines] = (
                (proj[:, at : at + PAIR].astype(F32) * HEAD_DIM**-0.5).T.astype(BF16)
            )
        k_out[lines, :] = proj[:, half : 2 * half]
        v_out[lines, :] = proj[:, 2 * half :]


def project(blocks, own, oth, bias, pieces):
    rows, width = own.shape
    seq = 2 * rows
    columns = bias.shape[1]
    half = columns // 3
    shape = jax.ShapeDtypeStruct
    return pl.pallas_call(
        functools.partial(project_kernel, len(pieces)),
        in_specs=[SCALARS, WHOLE, WHOLE, WHOLE] + [LEFT] * len(pieces),
        out_specs=[WHOLE] * 3,
        out_shape=[shape((half, seq), BF16), shape((seq, half), BF16), shape((seq, half), BF16)],
        scratch_shapes=[pltpu.VMEM((width, columns), BF16), pltpu.SemaphoreType.DMA((16,))],
        compiler_params=params(),
        cost_estimate=cost(2 * seq * width * columns, 6 << 20),
        name="project",
    )(blocks, own, oth, bias, *pieces)


def attend_kernel(q_ref, k_ref, v_ref, extra, ctx_a, ctx_b, ctx_t, lse_out):
    rows = ctx_a.shape[0]
    seq = k_ref.shape[0]
    q_t = q_ref[...].astype(F32)
    v_t = v_ref[...].astype(F32).T
    k_aug = jnp.concatenate([k_ref[...], extra[...]], axis=1)
    tail_row = lax.broadcasted_iota(jnp.int32, (PAIR, seq), 0)
    tail = jnp.where(tail_row == 3, 1.0, 0.0).astype(BF16)
    step = min(256, seq)
    q_augs, v_augs = [], []
    for head in range(2):
        mine = head_rows((PAIR, seq), head)
        q_augs.append(
            jnp.concatenate([jnp.where(mine, q_t, 0.0).astype(BF16), tail], axis=0)
        )
        v_augs.append(jnp.where(mine, v_t, 1.0).astype(BF16))
    work = [(head, at) for head in range(2) for at in range(0, seq, step)]

    def scores_of(head, at):
        return dot(k_aug, q_augs[head][:, at : at + step])

    following = scores_of(*work[0])
    for place, (head, at) in enumerate(work):
        scores = following
        if place + 1 < len(work):
            following = scores_of(*work[place + 1])
        top = jnp.max(scores, axis=0, keepdims=True)
        expo = jnp.exp(scores - top).astype(BF16)
        both = dot(v_augs[head], expo)
        own_at, oth_at = head * HEAD_DIM, (1 - head) * HEAD_DIM
        total = both[oth_at : oth_at + HEAD_DIM]
        ctx_t[own_at : own_at + HEAD_DIM, at : at + step] = (
            both[own_at : own_at + HEAD_DIM] / total
        ).astype(BF16)
        lse_out[head : head + 1, at : at + step] = top + jnp.log(total[0:1])
    turned = ctx_t[...].astype(F32).T.astype(BF16)
    ctx_a[...] = turned[:rows]
    ctx_b[...] = turned[rows:]


def pair_specs(first, seq):
    wide = pl.BlockSpec((PAIR, seq), lambda i: (first + i, 0))
    tall = pl.BlockSpec((seq, PAIR), lambda i: (0, first + i))
    tall_half = pl.BlockSpec((seq // 2, PAIR), lambda i: (0, first + i))
    return wide, tall, tall_half


def attend(first, last, q_t, keyed, valued, extra):
    seq = keyed.shape[0]
    count = last - first
    wide, tall, _ = pair_specs(first, seq)
    own_wide, _, own_half = pair_specs(0, seq)
    shape = jax.ShapeDtypeStruct
    return pl.pallas_call(
        attend_kernel,
        grid=(count,),
        in_specs=[wide, tall, tall, WHOLE],
        out_specs=[own_half, own_half, own_wide, pl.BlockSpec((8, seq), lambda i: (i, 0))],
        out_shape=[
            shape((seq // 2, count * PAIR), BF16),
            shape((seq // 2, count * PAIR), BF16),
            shape((count * PAIR, seq), BF16),
            shape((count * 8, seq), F32),
        ],
        compiler_params=params(),
        cost_estimate=cost(64 * count * seq * seq * PAIR, 2 << 20, count * seq * seq * 2),
        name="attend",
    )(q_t, keyed, valued, extra)


def three_parts(value):
    high = value.astype(BF16).astype(F32)
    mid = (value - high).astype(BF16).astype(F32)
    return high, mid, value - high - mid


def attend_back_kernel(q_t, keyed, valued, ctx_t, lse, d_a, d_b, extra, dq, dk, dv, sums, d_qt):
    seq = keyed.shape[0]
    tail_row = lax.broadcasted_iota(jnp.int32, (PAIR, seq), 0)

    def tail(parts, mask):
        rows = jnp.where(tail_row == 3, mask, 0.0)
        for place, part in enumerate(parts):
            rows = jnp.where(tail_row == place, part, rows)
        return rows.astype(BF16)

    d_t = jnp.concatenate([d_a[...].astype(F32).T, d_b[...].astype(F32).T], axis=1)
    q_full = q_t[...].astype(F32)
    product = d_t * ctx_t[...].astype(F32)
    k_aug = jnp.concatenate([keyed[...], extra[...]], axis=1)
    v_aug = jnp.concatenate([valued[...], extra[...]], axis=1)
    k_t = keyed[...].astype(F32).T.astype(BF16)
    step = min(256, seq)
    q_heads, d_heads, q_augs, d_augs = [], [], [], []
    for head in range(2):
        mine = head_rows((PAIR, seq), head)
        delta = jnp.sum(
            product[head * HEAD_DIM : (head + 1) * HEAD_DIM], axis=0, keepdims=True
        )
        q_heads.append(jnp.where(mine, q_full, 0.0).astype(BF16))
        d_heads.append(jnp.where(mine, d_t, 0.0).astype(BF16))
        q_augs.append(
            jnp.concatenate([q_heads[head], tail(three_parts(-lse[head : head + 1, :]), 1.0)], axis=0)
        )
        d_augs.append(jnp.concatenate([d_heads[head], tail(three_parts(-delta), 0.0)], axis=0))
    work = [(at, head) for at in range(0, seq, step) for head in range(2)]

    def products(at, head):
        keys = slice(at, at + step)
        return dot(k_aug[keys], q_augs[head]), dot(v_aug[keys], d_augs[head])

    following = products(*work[0])
    key_sum = value_sum = None
    for place, (at, head) in enumerate(work):
        keys = slice(at, at + step)
        scores, d_probs = following
        if place + 1 < len(work):
            following = products(*work[place + 1])
        probs = jnp.exp(scores)
        d_scores = (probs * d_probs).astype(BF16)
        part = dot(probs.astype(BF16), d_heads[head], 1, 1)
        value_sum = part if head == 0 else value_sum + part
        part = dot(d_scores, q_heads[head], 1, 1)
        key_sum = part if head == 0 else key_sum + part
        lines = slice(head * HEAD_DIM, (head + 1) * HEAD_DIM)
        part = dot(k_t[lines, keys], d_scores)
        if at == 0:
            d_qt[lines, :] = part
        else:
            d_qt[lines, :] += part
        if head == 1:
            dk[keys, :] = key_sum.astype(BF16)
            dv[keys, :] = value_sum.astype(BF16)
    dq[...] = (d_qt[...] * HEAD_DIM**-0.5).T.astype(BF16)
    sums[...] = jnp.zeros(sums.shape, F32)
    sums[0:1, :] = jnp.sum(dq[...].astype(F32), axis=0, keepdims=True)
    sums[1:2, :] = jnp.sum(dv[...].astype(F32), axis=0, keepdims=True)


def attend_back(first, last, q_t, keyed, valued, ctx_t, lse, d_a, d_b, extra):
    seq = keyed.shape[0]
    count = last - first
    wide, tall, tall_half = pair_specs(first, seq)
    own_wide, own_tall, _ = pair_specs(0, seq)
    shape = jax.ShapeDtypeStruct
    return pl.pallas_call(
        attend_back_kernel,
        grid=(count,),
        in_specs=[
            wide,
            tall,
            tall,
            own_wide,
            pl.BlockSpec((8, seq), lambda i: (i, 0)),
            tall_half,
            tall_half,
            WHOLE,
        ],
        out_specs=[own_tall] * 3 + [pl.BlockSpec((8, PAIR), lambda i: (0, i))],
        out_shape=[shape((seq, count * PAIR), BF16)] * 3 + [shape((8, count * PAIR), F32)],
        scratch_shapes=[pltpu.VMEM((PAIR, seq), F32)],
        compiler_params=params(),
        cost_estimate=cost(64 * count * seq * seq * PAIR, 3 << 20, count * seq * seq * 2),
        name="attend_back",
    )(q_t, keyed, valued, ctx_t, lse, d_a, d_b, extra)


def row_mean(value):
    return jnp.mean(value, axis=1, keepdims=True)


def normed(value):
    centred = value - row_mean(value)
    rate = lax.rsqrt(row_mean(centred * centred) + EPS)
    return centred * rate, rate


def norm_back(grad, hat, rate, gain):
    scaled = grad * gain
    return rate * (scaled - row_mean(scaled) - hat * row_mean(scaled * hat))


def column_sum(value):
    return jnp.sum(value, axis=0, keepdims=True)


def gelu(value):
    phi = 0.5 + 0.5 * lax.erf(value * (0.5**0.5))
    return phi, jnp.exp(value * value * -0.5) * (1.0 / math.sqrt(2.0 * math.pi))


def hidden_spans(hidden, chunk):
    return [(side, at, side * hidden + at) for side in range(2) for at in range(0, hidden, chunk)]


CHUNK = 512


def middle_kernel(count, parts, blocks, *rest):
    ctx_parts = rest[:parts]
    ctx_oth, x_ref, cot_ref, vectors, b_up = rest[parts : parts + 5]
    rest = rest[parts + 5 :]
    pieces = [rest[at : at + count] for at in range(0, 4 * count, count)]
    rest = rest[4 * count :]
    out, dz, dctx_own, dctx_oth, sums, sent_f, kept_f, sent_d, kept_d = rest[:9]
    w_own, w_oth, down_own, down_oth = rest[9:13]
    ctx_s, x_s, cot_s, act_s, slope_s, y_t, d_t, dz_t = rest[13:21]
    out_s, dz_s, dctx_s, tile, got_f, got_d, sems = rest[21:]
    wholes, downs = (w_own, w_oth), (down_own, down_oth)
    half = ctx_oth.shape[1]
    hidden = down_own.shape[1]
    width = x_ref.shape[1]
    mover = Mover(sems)
    stores = []

    inputs, at = [], 0
    for part in ctx_parts:
        size = part.shape[1]
        inputs.append(mover.start(part, ctx_s.at[0, :, pl.ds(at, size)]))
        at += size
    inputs.append(mover.start(ctx_oth, ctx_s.at[1]))
    loads = []
    for span in ((0, half), (half, hidden)):
        for side in range(2):
            loads.append(load_weight(mover, blocks, side, pieces[side], wholes[side], *span))
    for side in range(2):
        loads.append(load_weight(mover, blocks, side, pieces[2 + side], downs[side]))
    for place, load in enumerate(loads):
        for copy in load:
            copy.start()
        if place == 1:
            inputs.append(mover.start(x_ref, x_s))
    late = mover.start(cot_ref, cot_s)
    wait(inputs + loads[0] + loads[1])

    def put(tiles, lefts, rights, side, held, out_ref):
        for left, right, at, size, column in tiles:
            tile[:, :size] = dot(lefts[left][...], rights[right][:, at : at + size]).astype(BF16)
            store_pieces(blocks, [held], column, tile.at[:, pl.ds(0, size)], side)
            span = pl.ds(column, size)
            stores.append(mover.start(held.at[:, :, span], out_ref.at[:, :, span]))

    b_out, gain_one, shift_one = vectors[0:1, :], vectors[1:2, :], vectors[2:3, :]
    b_down, gain_two, shift_two = vectors[3:4, :], vectors[4:5, :], vectors[5:6, :]
    attn = dot(ctx_s[0], w_own[:, :half], 1, 1) + dot(ctx_s[1], w_oth[:, :half], 1, 1)
    hat_one, rate_one = normed(attn + b_out + x_s[...].astype(F32))
    y_one = hat_one * gain_one + shift_one
    low = y_one.astype(BF16)
    spans = hidden_spans(hidden, CHUNK)
    ffn = None
    wait(loads[2] + loads[3])

    def pre_of(side, at, _):
        pre = dot(low, wholes[side][:, half + at : half + at + CHUNK])
        return pre + b_up[side : side + 1, at : at + CHUNK]

    following = pre_of(*spans[0])
    for number, (side, at, place) in enumerate(spans):
        pre = following
        if number + 1 < len(spans):
            following = pre_of(*spans[number + 1])
        phi, bell = gelu(pre)
        act = (pre * phi).astype(BF16)
        act_s[:, place : place + CHUNK] = act
        slope_s[:, place : place + CHUNK] = (phi + pre * bell).astype(BF16)
        if number == 0:
            wait(loads[4] + loads[5])
        part = dot(act, downs[side][:, at : at + CHUNK], 1, 1)
        ffn = part if ffn is None else ffn + part
    hat_two, rate_two = normed(ffn + b_down + y_one)
    out_s[...] = (hat_two * gain_two + shift_two).astype(BF16)
    stores.append(mover.start(out_s, out))
    late.wait()
    cot = cot_s[...].astype(F32)
    d_two = norm_back(cot, hat_two, rate_two, gain_two)
    d_ffn = d_two.astype(BF16)
    d_t[...] = d_two.T.astype(BF16)
    y_t[...] = y_one.T.astype(BF16)
    sums[3:4, :] = column_sum(d_two)
    sums[4:5, :] = column_sum(cot * hat_two)
    sums[5:6, :] = column_sum(cot)
    for side, (held, out_ref) in ((1, (got_d.at[1], sent_d)), (0, (got_d.at[0], kept_d))):
        tiles = [(0, 0, side * hidden + at, CHUNK, at) for at in range(0, hidden, CHUNK)]
        put(tiles, [d_t], [act_s], side, held, out_ref)
    back = None

    def d_act_of(side, at, _):
        return dot(d_ffn, downs[side][:, at : at + CHUNK])

    following = d_act_of(*spans[0])
    for number, (side, at, place) in enumerate(spans):
        d_act = following
        if number + 1 < len(spans):
            following = d_act_of(*spans[number + 1])
        d_pre = (d_act * slope_s[:, place : place + CHUNK].astype(F32)).astype(BF16)
        slope_s[:, place : place + CHUNK] = d_pre
        total = column_sum(d_pre.astype(F32))
        for col in range(0, CHUNK, 256):
            spot = place + col
            row, left = 6 + spot // width, spot % width
            sums[row : row + 1, left : left + 256] = total[:, col : col + 256]
        part = dot(d_pre, wholes[side][:, half + at : half + at + CHUNK], 1, 1)
        back = part if back is None else back + part
    d_one = d_two + back
    d_zero = norm_back(d_one, hat_one, rate_one, gain_one)
    dz_s[...] = d_zero
    stores.append(mover.start(dz_s, dz))
    d_attn = d_zero.astype(BF16)
    dctx_s[0] = dot(d_attn, w_own[:, :half]).astype(BF16)
    dctx_s[1] = dot(d_attn, w_oth[:, :half]).astype(BF16)
    stores.append(mover.start(dctx_s.at[0], dctx_own))
    stores.append(mover.start(dctx_s.at[1], dctx_oth))
    dz_t[...] = d_zero.T.astype(BF16)
    sums[0:1, :] = column_sum(d_zero)
    sums[1:2, :] = column_sum(d_one * hat_one)
    sums[2:3, :] = column_sum(d_one)
    for side, (held, out_ref) in ((1, (got_f.at[1], sent_f)), (0, (got_f.at[0], kept_f))):
        tiles = [
            (1, 1, side * hidden + at, CHUNK, half + at) for at in range(0, hidden, CHUNK)
        ] + [(0, 0, 0, half, 0)]
        put(tiles, [dz_t, y_t], [ctx_s.at[side], slope_s], 2 + side, held, out_ref)
    wait(stores)


def middle(blocks, ctx_parts, ctx_oth, own, cotangent, vectors, b_up, pieces):
    rows, width = own.shape
    half = ctx_oth.shape[1]
    hidden = b_up.shape[1]
    shape = jax.ShapeDtypeStruct
    count = len(pieces[0])
    sum_rows = 6 + 2 * hidden // width
    flops = 2 * rows * width * (6 * half + 12 * hidden)
    number = blocks.shape[1]
    first = (number, width // number, half + hidden)
    down = (number, width // number, hidden)
    vmem = pltpu.VMEM
    return pl.pallas_call(
        functools.partial(middle_kernel, count, len(ctx_parts)),
        in_specs=[SCALARS]
        + [LEFT] * (len(ctx_parts) + 3)
        + [WHOLE, WHOLE]
        + [LEFT] * (4 * count),
        out_specs=[LEFT] * 4 + [WHOLE] + [LEFT] * 4,
        out_shape=[
            shape((rows, width), BF16),
            shape((rows, width), F32),
            shape((rows, half), BF16),
            shape((rows, half), BF16),
            shape((sum_rows, width), F32),
            shape(first, BF16),
            shape(first, BF16),
            shape(down, BF16),
            shape(down, BF16),
        ],
        scratch_shapes=[vmem((width, half + hidden), BF16)] * 2
        + [vmem((width, hidden), BF16)] * 2
        + [
            vmem((2, rows, half), BF16),
            vmem((rows, width), BF16),
            vmem((rows, width), BF16),
            vmem((rows, 2 * hidden), BF16),
            vmem((rows, 2 * hidden), BF16),
            vmem((width, rows), BF16),
            vmem((width, rows), BF16),
            vmem((width, rows), BF16),
            vmem((rows, width), BF16),
            vmem((rows, width), F32),
            vmem((2, rows, half), BF16),
            vmem((width, CHUNK), BF16),
            vmem((2, *first), BF16),
            vmem((2, *down), BF16),
            pltpu.SemaphoreType.DMA((144,)),
        ],
        compiler_params=params(),
        cost_estimate=cost(flops, 28 << 20, rows * hidden * 4),
        name="middle",
    )(
        blocks,
        *ctx_parts,
        ctx_oth,
        own,
        cotangent,
        vectors,
        b_up,
        *[piece for group in pieces for piece in group],
    )


def pair_places(parts):
    return [
        (group, at) for group, part in enumerate(parts) for at in range(0, part[0].shape[1], PAIR)
    ]


def grad_qkv_kernel(groups, blocks, x_t, *refs):
    parts = [refs[3 * group : 3 * group + 3] for group in range(groups)]
    refs = refs[3 * groups :]
    x_s, right_s, tile, sems = refs[-4:]
    outs, held = refs[:-6], refs[-6:-4]
    held = held[: len(outs)]
    mover = Mover(sems)
    loads = [mover.start(x_t, x_s)]
    places = pair_places(parts)
    for pair, (group, at) in enumerate(places):
        loads.append(
            [
                mover.start(
                    part.at[:, pl.ds(at, PAIR)], right_s.at[pair, :, pl.ds(kind * PAIR, PAIR)]
                )
                for kind, part in enumerate(parts[group])
            ]
        )
    loads[0].wait()
    stores = []
    for pair in range(len(places)):
        wait(loads[1 + pair])
        tile[...] = dot(x_s[...], right_s[pair]).astype(BF16)
        column = 3 * PAIR * pair
        store_pieces(blocks, held, column, tile)
        span = pl.ds(column, 3 * PAIR)
        for mine, out in zip(held, outs):
            stores.append(mover.start(mine.at[:, :, span], out.at[:, :, span]))
    wait(stores)


def grad_qkv_pieces(blocks, x_t, d_parts):
    width, seq = x_t.shape
    flat = [part for parts in d_parts for part in parts]
    columns = sum(part.shape[1] for part in flat)
    shapes = piece_shapes(blocks.shape[1], width, columns)
    held = [pltpu.VMEM(one.shape, BF16) for one in shapes]
    held += [pltpu.VMEM((8, 128), BF16)] * (2 - len(held))
    return pl.pallas_call(
        functools.partial(grad_qkv_kernel, len(d_parts)),
        in_specs=[SCALARS] + [LEFT] * (1 + len(flat)),
        out_specs=[LEFT] * len(shapes),
        out_shape=shapes,
        scratch_shapes=held
        + [
            pltpu.VMEM((width, seq), BF16),
            pltpu.VMEM((columns // (3 * PAIR), seq, 3 * PAIR), BF16),
            pltpu.VMEM((width, 3 * PAIR), BF16),
            pltpu.SemaphoreType.DMA((32,)),
        ],
        compiler_params=params(),
        cost_estimate=cost(2 * seq * width * columns, 6 << 20),
        name="grad_qkv",
    )(blocks, x_t, *flat)


def input_kernel(count, groups, blocks, *refs):
    parts = [refs[3 * group : 3 * group + 3] for group in range(groups)]
    refs = refs[3 * groups :]
    dz, pieces = refs[0], refs[1 : 1 + count]
    kept, sent, weight, whole, dz_s, sent_s, sems = refs[1 + count :]
    mover = Mover(sems)
    rows = kept.shape[0]
    half = whole.shape[1] // 3
    loads = load_weight(mover, blocks, 0, pieces, weight)
    for pair, (group, at) in enumerate(pair_places(parts)):
        for kind, part in enumerate(parts[group]):
            target = whole.at[:, pl.ds(kind * half + pair * PAIR, PAIR)]
            loads.append(mover.copy(part.at[:, pl.ds(at, PAIR)], target))
    for copy in loads:
        copy.start()
    last = mover.start(dz, dz_s)
    wait(loads)
    sent_s[...] = dot(whole[rows:, :], weight[...], 1, 1).astype(BF16)
    store = mover.start(sent_s, sent)
    last.wait()
    dz_s[...] += dot(whole[:rows, :], weight[...], 1, 1)
    mover.start(dz_s, kept).wait()
    store.wait()


def input_grad(blocks, d_parts, dz, pieces):
    rows, width = dz.shape
    flat = [part for parts in d_parts for part in parts]
    columns = sum(part.shape[1] for part in flat)
    shape = jax.ShapeDtypeStruct
    return pl.pallas_call(
        functools.partial(input_kernel, len(pieces), len(d_parts)),
        in_specs=[SCALARS] + [LEFT] * (len(flat) + 1 + len(pieces)),
        out_specs=[LEFT] * 2,
        out_shape=[shape((rows, width), F32), shape((rows, width), BF16)],
        scratch_shapes=[
            pltpu.VMEM((width, columns), BF16),
            pltpu.VMEM((2 * rows, columns), BF16),
            pltpu.VMEM((rows, width), F32),
            pltpu.VMEM((rows, width), BF16),
            pltpu.SemaphoreType.DMA((48,)),
        ],
        compiler_params=params(),
        cost_estimate=cost(4 * rows * width * columns, 8 << 20),
        name="input_grad",
    )(blocks, *flat, dz, *pieces)


def per_device(
    layer_in,
    seq_lens,
    w_qkv,
    b_qv,
    w_out,
    b_out,
    gain_one,
    shift_one,
    w_up,
    b_up,
    w_down,
    b_down,
    gain_two,
    shift_two,
    cotangent,
):
    rows, width = layer_in.shape
    seq = 2 * rows
    side = lax.axis_index("tensor")
    shard_rows, _, half = w_qkv.shape
    hidden = w_up.shape[1]
    blocks = row_blocks(side)
    pairs = range(half // PAIR)

    gather_qkv = Gather(w_qkv.reshape(shard_rows, 3 * half))
    gather_first = Gather(jnp.concatenate([w_out, w_up], axis=1))
    gather_down = Gather(w_down)
    oth_in = swap(layer_in)
    qkv_0 = gather_qkv.step()
    gather_first.step(qkv_0)
    qkv_1 = gather_qkv.step()
    gather_first.step(qkv_1)
    qkv_2 = gather_qkv.step()
    gather_down.step(qkv_2)
    qkv_3 = gather_qkv.step()
    gather_first.step(qkv_3)
    x_t = jnp.concatenate([after(layer_in, qkv_0), oth_in], axis=0).T

    bias_qv = lax.dynamic_slice_in_dim(b_qv, side * half, half, 1)
    bias = jnp.concatenate([bias_qv[0:1], jnp.zeros((1, half), F32), bias_qv[1:2]], axis=1)
    row = jnp.arange(seq, dtype=jnp.int32)
    position = ((row // rows) ^ side) * rows + row % rows
    lane = jnp.arange(PAIR, dtype=jnp.int32)[None, :]
    masked = jnp.where(position < seq_lens[0], 0.0, NEG)[:, None]
    extra = jnp.where(lane < 3, 1.0, jnp.where(lane == 3, masked, 0.0)).astype(BF16)

    q_t, keyed, valued = project(blocks, layer_in, oth_in, bias, gather_qkv.pieces)
    gather_down.step(qkv_3)
    gather_first.step()
    gather_down.step(q_t)
    first_pieces, down_pieces = gather_first.pieces, gather_down.pieces
    attended = [
        attend(0, 1, after(q_t, gather_first.sent), keyed, valued, extra)
    ]
    gather_down.step(attended[0][3])
    down_pieces = gather_down.pieces
    first_oth = [swap(after(first_pieces[0], attended[0][3]))]
    attended.append(
        attend(1, 2, after(q_t, attended[0][3], gather_down.sent), keyed, valued, extra)
    )
    first_oth += [swap(after(piece, attended[1][3])) for piece in first_pieces[1:]]
    down_oth = [swap(after(down_pieces[0], attended[1][3]))]
    attended.append(attend(2, 3, after(q_t, attended[1][3]), keyed, valued, extra))
    down_oth += [swap(after(piece, attended[2][3])) for piece in down_pieces[1:]]
    ctx_parts = [one[0] for one in attended]
    ctx_oth = swap(jnp.concatenate([one[1] for one in attended], axis=1))
    up_parts = b_up.reshape(2, hidden)
    up_bias = jnp.where(side == 0, up_parts, up_parts[::-1])
    vectors = jnp.stack([b_out, gain_one, shift_one, b_down, gain_two, shift_two])
    output, dz, dctx_own, dctx_oth, sums, sent_f, kept_f, sent_d, kept_d = middle(
        blocks,
        ctx_parts,
        ctx_oth,
        layer_in,
        cotangent,
        vectors,
        up_bias,
        [first_pieces, first_oth, down_pieces, down_oth],
    )
    d_ctx_b = swap(dctx_oth)
    scatter_down = Scatter([kept_d, swap(sent_d)], added=True)
    scatter_first = Scatter([kept_f, swap(sent_f)], 1, added=True)

    up_rows = hidden // width

    def back(group, first, last, *others):
        ctx_t, lse = attended[group][2:]
        return attend_back(
            first, last, after(q_t, *others), keyed, valued, ctx_t, lse, dctx_own, d_ctx_b, extra
        )

    backs = [back(0, 0, 1)]
    scatter_down.step(backs[0][3])
    first_3 = scatter_first.step(backs[0][3])
    backs.append(back(1, 1, 2, backs[0][3], scatter_down.sent, scatter_first.sent))
    scatter_down.step(backs[1][3])
    backs.append(back(2, 2, 3, backs[1][3], scatter_down.sent))
    d_parts = [one[:3] for one in backs]
    qkv_kept = grad_qkv_pieces(blocks, x_t, d_parts)
    qv = jnp.concatenate([one[3][:2] for one in backs], axis=1).reshape(1, 2 * half)
    small = jnp.concatenate([sums, qv], axis=0)
    small = jnp.pad(small, ((0, 16 - small.shape[0]), (0, 0)))
    scatter_qkv = Scatter(qkv_kept, extra=small)
    scatter_qkv.step()
    scatter_down.step(qkv_kept[0])
    kept, sent = input_grad(
        blocks, d_parts, after(dz, qkv_kept[0]), gather_qkv.pieces
    )
    first_2 = scatter_first.step(kept)
    oth_dx = swap(sent)
    qkv_2 = scatter_qkv.step(scatter_first.sent)
    scatter_first.step(kept)
    scatter_down.step(kept)
    grad_input = (kept + oth_dx.astype(F32)).astype(BF16)
    scatter_qkv.step(first_2)
    scatter_first.step(qkv_2)
    scatter_qkv.step()
    both = scatter_qkv.extra
    oth = swap(both)
    norms = both[:6] + oth[:6]
    grad_bup = both[6 : 6 + up_rows] + oth[6 + up_rows : 6 + 2 * up_rows]
    grad_bqv = both[6 + 2 * up_rows].reshape(2, half)
    grad_qkv = scatter_qkv.result().reshape(shard_rows, half // PAIR, 3, PAIR).transpose(0, 2, 1, 3)
    grad_first, grad_down = scatter_first.result(), scatter_down.result()

    return (
        output,
        grad_input,
        grad_qkv.reshape(shard_rows, 3, half),
        grad_bqv,
        grad_first[:, :half],
        norms[0],
        norms[1],
        norms[2],
        grad_first[:, half:],
        grad_bup.reshape(hidden),
        grad_down,
        norms[3],
        norms[4],
        norms[5],
    )


def solution(mesh):
    placed = (
        P(("dp", "tensor"), None),
        P("dp"),
        P("dp", None, "tensor"),
        P(),
        P("dp", "tensor"),
        P(),
        P(),
        P(),
        P("dp", "tensor"),
        P(),
        P("dp", "tensor"),
        P(),
        P(),
        P(),
        P(("dp", "tensor"), None),
    )
    return jax.shard_map(
        per_device,
        mesh=mesh,
        in_specs=placed,
        out_specs=(
            P(("dp", "tensor"), None),
            P(("dp", "tensor"), None),
            P("dp", None, "tensor"),
            P(None, "tensor"),
            P("dp", "tensor"),
            P(),
            P(),
            P(),
            P("dp", "tensor"),
            P("tensor"),
            P("dp", "tensor"),
            P(),
            P(),
            P(),
        ),
        check_vma=False,
    )
```

```python
import functools
import math

import jax
import jax.numpy as jnp
from jax import lax
from jax.experimental import pallas as pl
from jax.experimental.pallas import tpu as pltpu
from jax.sharding import PartitionSpec as P

HEAD_DIM = 64
PAIR = 2 * HEAD_DIM
EPS = 1e-05
NEG = -1e30
F32 = jnp.float32
BF16 = jnp.bfloat16
VMEM_LIMIT = 60 << 20


def dot(left, right, left_dim=1, right_dim=0):
    return lax.dot_general(
        left, right, (((left_dim,), (right_dim,)), ((), ())), preferred_element_type=F32
    )


def params(**more):
    return pltpu.CompilerParams(vmem_limit_bytes=VMEM_LIMIT, **more)


def cost(flops, size, trans=0):
    return pl.CostEstimate(
        flops=int(flops) // 10, bytes_accessed=int(size) // 10, transcendentals=int(trans) // 10
    )


WHOLE = pl.BlockSpec(memory_space=pltpu.VMEM)
SCALARS = pl.BlockSpec(memory_space=pltpu.SMEM)
LEFT = pl.BlockSpec(memory_space=pl.ANY)


def swap(value):
    return lax.ppermute(value, "tensor", [(0, 1), (1, 0)])


def by_hops():
    return lax.axis_size("dp") == 16


ORDERS = (((8, 4, 1, 2), (2, 8, 4, 1)), ((8, 4, 2, 1), (1, 8, 4, 2)))


def offsets(kind, core):
    found = [0]
    for step in ORDERS[kind][core]:
        found += [one ^ step for one in found]
    return found


def hop(value, level, kind):
    pairs = [
        (2 * device + core, 2 * (device ^ ORDERS[kind][core][level]) + core)
        for device in range(16)
        for core in range(2)
    ]
    return lax.ppermute(value, ("dp", "tensor"), pairs)


def row_blocks(side):
    if not by_hops():
        return jnp.zeros((4, 1), jnp.int32)
    tables = [
        jnp.array([offsets(kind, core) for kind in range(2) for core in order], jnp.int32)
        for order in ((0, 1), (1, 0))
    ]
    return lax.axis_index("dp").astype(jnp.int32) ^ jnp.where(side == 0, *tables)


def after(value, *others):
    return lax.optimization_barrier((value, others))[0] if others else value


class Gather:
    def __init__(self, shard, kind=0):
        self.held = shard[None]
        self.level = 0
        self.kind = kind

    def step(self, *others):
        held = self.sent = after(self.held, *others)
        if not by_hops():
            if self.level == 0:
                self.pieces = [lax.all_gather(held[0], "dp", axis=0, tiled=True)[None]]
            self.level += 1
            return self.pieces[0]
        got = hop(held, self.level, self.kind)
        self.level += 1
        if self.level < 4:
            self.held = jnp.concatenate([held, got], axis=0)
        self.pieces = [held, got]
        return got


class Scatter:
    def __init__(self, pieces, kind=0, added=False, extra=None):
        self.parts = list(pieces)
        self.kind = kind
        self.level = 4
        self.added = added
        self.extra = extra

    def extra_block(self, columns):
        high = lax.reduce_precision(self.extra, 8, 7)
        mid = lax.reduce_precision(self.extra - high, 8, 7)
        block = jnp.concatenate([high, mid, self.extra - high - mid], axis=0).astype(BF16)
        return jnp.pad(block, ((0, 0), (0, columns - block.shape[1])))[None]

    def add_extra(self, block):
        rows, width = self.extra.shape
        high, mid, low = [
            block[at : at + rows, :width].astype(F32) for at in range(0, 3 * rows, rows)
        ]
        self.extra = self.extra + ((high + mid) + low)

    def total(self, at):
        return functools.reduce(lambda a, b: a + b, [part[at].astype(F32) for part in self.parts])

    def step(self, *others):
        self.level -= 1
        if not by_hops():
            if self.level == 3:
                whole = after(self.parts[0][0], *others).astype(F32)
                if self.added:
                    whole = whole + self.parts[1][0].astype(F32)
                self.sums = lax.psum_scatter(whole, "dp", scatter_dimension=0, tiled=True)
                if self.extra is not None:
                    self.extra = lax.psum(self.extra, "dp")
            self.sent = self.sums
            return self.sums
        if self.level == 3 and not self.added:
            self.parts, sent = self.parts[:1], self.parts[1]
        else:
            size = 1 << self.level
            sent = self.total(slice(size, 2 * size)).astype(BF16)
        if self.extra is not None:
            sent = jnp.concatenate([sent, self.extra_block(sent.shape[2])], axis=0)
        self.sent = after(sent, *others)
        got = hop(self.sent, self.level, self.kind)
        if self.extra is not None:
            self.add_extra(got[-1])
        self.parts.append(got)
        return got

    def result(self):
        return self.total(0) if by_hops() else self.sums


class Mover:
    def __init__(self, sems):
        self.sems = sems
        self.count = 0

    def copy(self, source, target):
        made = pltpu.make_async_copy(source, target, self.sems.at[self.count])
        self.count += 1
        return made

    def start(self, source, target):
        made = self.copy(source, target)
        made.start()
        return made


def wait(copies):
    for copy in copies:
        copy.wait()


def load_weight(mover, blocks, side, pieces, whole, start=0, size=None):
    copies = []
    size = whole.shape[1] if size is None else size
    columns = pl.ds(start, size)
    for piece in pieces:
        rows = piece.shape[1]
        for sub in range(piece.shape[0]):
            at = pl.multiple_of(blocks[side, len(copies)] * rows, 16)
            copies.append(
                mover.copy(piece.at[sub, :, columns], whole.at[pl.ds(at, rows), columns])
            )
    return copies


def store_pieces(blocks, outs, column, tile, side=0):
    place = 0
    for out in outs:
        rows = out.shape[1]
        for sub in range(out.shape[0]):
            at = pl.multiple_of(blocks[side, place] * rows, 16)
            out[sub, :, column : column + tile.shape[1]] = tile[pl.ds(at, rows), :]
            place += 1


def piece_shapes(blocks, rows, columns):
    if blocks == 1:
        return [jax.ShapeDtypeStruct((1, rows, columns), BF16)]
    return [jax.ShapeDtypeStruct((blocks // 2, rows // blocks, columns), BF16)] * 2


def head_rows(shape, head):
    row = lax.broadcasted_iota(jnp.int32, shape, 0)
    return (row >= head * HEAD_DIM) & (row < (head + 1) * HEAD_DIM)


def project_kernel(count, blocks, own, oth, bias, *rest):
    pieces = rest[:count]
    q_out, k_out, v_out, weight, sems = rest[count:]
    half = weight.shape[1] // 3
    rows = own.shape[0]
    copies = load_weight(Mover(sems), blocks, 0, pieces, weight)
    for copy in copies:
        copy.start()
    wait(copies)
    for place, ref in enumerate((own, oth)):
        lines = slice(place * rows, (place + 1) * rows)
        proj = (dot(ref[...], weight[...]) + bias[...]).astype(BF16)
        for at in range(0, half, PAIR):
            q_out[at : at + PAIR, lines] = (
                (proj[:, at : at + PAIR].astype(F32) * HEAD_DIM**-0.5).T.astype(BF16)
            )
        k_out[lines, :] = proj[:, half : 2 * half]
        v_out[lines, :] = proj[:, 2 * half :]


def project(blocks, own, oth, bias, pieces):
    rows, width = own.shape
    seq = 2 * rows
    columns = bias.shape[1]
    half = columns // 3
    shape = jax.ShapeDtypeStruct
    return pl.pallas_call(
        functools.partial(project_kernel, len(pieces)),
        in_specs=[SCALARS, WHOLE, WHOLE, WHOLE] + [LEFT] * len(pieces),
        out_specs=[WHOLE] * 3,
        out_shape=[shape((half, seq), BF16), shape((seq, half), BF16), shape((seq, half), BF16)],
        scratch_shapes=[pltpu.VMEM((width, columns), BF16), pltpu.SemaphoreType.DMA((16,))],
        compiler_params=params(),
        cost_estimate=cost(2 * seq * width * columns, 6 << 20),
        name="project",
    )(blocks, own, oth, bias, *pieces)


def attend_kernel(q_ref, k_ref, v_ref, extra, ctx_a, ctx_b, ctx_t, lse_out):
    rows = ctx_a.shape[0]
    seq = k_ref.shape[0]
    q_t = q_ref[...].astype(F32)
    v_t = v_ref[...].astype(F32).T
    k_aug = jnp.concatenate([k_ref[...], extra[...]], axis=1)
    tail_row = lax.broadcasted_iota(jnp.int32, (PAIR, seq), 0)
    tail = jnp.where(tail_row == 3, 1.0, 0.0).astype(BF16)
    step = min(256, seq)
    q_augs, v_augs = [], []
    for head in range(2):
        mine = head_rows((PAIR, seq), head)
        q_augs.append(
            jnp.concatenate([jnp.where(mine, q_t, 0.0).astype(BF16), tail], axis=0)
        )
        v_augs.append(jnp.where(mine, v_t, 1.0).astype(BF16))
    work = [(head, at) for head in range(2) for at in range(0, seq, step)]

    def scores_of(head, at):
        return dot(k_aug, q_augs[head][:, at : at + step])

    following = scores_of(*work[0])
    for place, (head, at) in enumerate(work):
        scores = following
        if place + 1 < len(work):
            following = scores_of(*work[place + 1])
        top = jnp.max(scores, axis=0, keepdims=True)
        expo = jnp.exp(scores - top).astype(BF16)
        both = dot(v_augs[head], expo)
        own_at, oth_at = head * HEAD_DIM, (1 - head) * HEAD_DIM
        total = both[oth_at : oth_at + HEAD_DIM]
        ctx_t[own_at : own_at + HEAD_DIM, at : at + step] = (
            both[own_at : own_at + HEAD_DIM] / total
        ).astype(BF16)
        lse_out[head : head + 1, at : at + step] = top + jnp.log(total[0:1])
    turned = ctx_t[...].astype(F32).T.astype(BF16)
    ctx_a[...] = turned[:rows]
    ctx_b[...] = turned[rows:]


def pair_specs(first, seq):
    wide = pl.BlockSpec((PAIR, seq), lambda i: (first + i, 0))
    tall = pl.BlockSpec((seq, PAIR), lambda i: (0, first + i))
    tall_half = pl.BlockSpec((seq // 2, PAIR), lambda i: (0, first + i))
    return wide, tall, tall_half


def attend(first, last, q_t, keyed, valued, extra):
    seq = keyed.shape[0]
    count = last - first
    wide, tall, _ = pair_specs(first, seq)
    own_wide, _, own_half = pair_specs(0, seq)
    shape = jax.ShapeDtypeStruct
    return pl.pallas_call(
        attend_kernel,
        grid=(count,),
        in_specs=[wide, tall, tall, WHOLE],
        out_specs=[own_half, own_half, own_wide, pl.BlockSpec((8, seq), lambda i: (i, 0))],
        out_shape=[
            shape((seq // 2, count * PAIR), BF16),
            shape((seq // 2, count * PAIR), BF16),
            shape((count * PAIR, seq), BF16),
            shape((count * 8, seq), F32),
        ],
        compiler_params=params(),
        cost_estimate=cost(64 * count * seq * seq * PAIR, 2 << 20, count * seq * seq * 2),
        name="attend",
    )(q_t, keyed, valued, extra)


def three_parts(value):
    high = value.astype(BF16).astype(F32)
    mid = (value - high).astype(BF16).astype(F32)
    return high, mid, value - high - mid


def attend_back_kernel(q_t, keyed, valued, ctx_t, lse, d_a, d_b, extra, dq, dk, dv, sums, d_qt):
    seq = keyed.shape[0]
    tail_row = lax.broadcasted_iota(jnp.int32, (PAIR, seq), 0)

    def tail(parts, mask):
        rows = jnp.where(tail_row == 3, mask, 0.0)
        for place, part in enumerate(parts):
            rows = jnp.where(tail_row == place, part, rows)
        return rows.astype(BF16)

    d_t = jnp.concatenate([d_a[...].astype(F32).T, d_b[...].astype(F32).T], axis=1)
    q_full = q_t[...].astype(F32)
    product = d_t * ctx_t[...].astype(F32)
    k_aug = jnp.concatenate([keyed[...], extra[...]], axis=1)
    v_aug = jnp.concatenate([valued[...], extra[...]], axis=1)
    k_t = keyed[...].astype(F32).T.astype(BF16)
    step = min(256, seq)
    q_heads, d_heads, q_augs, d_augs = [], [], [], []
    for head in range(2):
        mine = head_rows((PAIR, seq), head)
        delta = jnp.sum(
            product[head * HEAD_DIM : (head + 1) * HEAD_DIM], axis=0, keepdims=True
        )
        q_heads.append(jnp.where(mine, q_full, 0.0).astype(BF16))
        d_heads.append(jnp.where(mine, d_t, 0.0).astype(BF16))
        q_augs.append(
            jnp.concatenate([q_heads[head], tail(three_parts(-lse[head : head + 1, :]), 1.0)], axis=0)
        )
        d_augs.append(jnp.concatenate([d_heads[head], tail(three_parts(-delta), 0.0)], axis=0))
    work = [(at, head) for at in range(0, seq, step) for head in range(2)]

    def products(at, head):
        keys = slice(at, at + step)
        return dot(k_aug[keys], q_augs[head]), dot(v_aug[keys], d_augs[head])

    following = products(*work[0])
    key_sum = value_sum = None
    for place, (at, head) in enumerate(work):
        keys = slice(at, at + step)
        scores, d_probs = following
        if place + 1 < len(work):
            following = products(*work[place + 1])
        probs = jnp.exp(scores)
        d_scores = (probs * d_probs).astype(BF16)
        part = dot(probs.astype(BF16), d_heads[head], 1, 1)
        value_sum = part if head == 0 else value_sum + part
        part = dot(d_scores, q_heads[head], 1, 1)
        key_sum = part if head == 0 else key_sum + part
        lines = slice(head * HEAD_DIM, (head + 1) * HEAD_DIM)
        part = dot(k_t[lines, keys], d_scores)
        if at == 0:
            d_qt[lines, :] = part
        else:
            d_qt[lines, :] += part
        if head == 1:
            dk[keys, :] = key_sum.astype(BF16)
            dv[keys, :] = value_sum.astype(BF16)
    dq[...] = (d_qt[...] * HEAD_DIM**-0.5).T.astype(BF16)
    sums[...] = jnp.zeros(sums.shape, F32)
    sums[0:1, :] = jnp.sum(dq[...].astype(F32), axis=0, keepdims=True)
    sums[1:2, :] = jnp.sum(dv[...].astype(F32), axis=0, keepdims=True)


def attend_back(first, last, q_t, keyed, valued, ctx_t, lse, d_a, d_b, extra):
    seq = keyed.shape[0]
    count = last - first
    wide, tall, tall_half = pair_specs(first, seq)
    own_wide, own_tall, _ = pair_specs(0, seq)
    shape = jax.ShapeDtypeStruct
    return pl.pallas_call(
        attend_back_kernel,
        grid=(count,),
        in_specs=[
            wide,
            tall,
            tall,
            own_wide,
            pl.BlockSpec((8, seq), lambda i: (i, 0)),
            tall_half,
            tall_half,
            WHOLE,
        ],
        out_specs=[own_tall] * 3 + [pl.BlockSpec((8, PAIR), lambda i: (0, i))],
        out_shape=[shape((seq, count * PAIR), BF16)] * 3 + [shape((8, count * PAIR), F32)],
        scratch_shapes=[pltpu.VMEM((PAIR, seq), F32)],
        compiler_params=params(),
        cost_estimate=cost(64 * count * seq * seq * PAIR, 3 << 20, count * seq * seq * 2),
        name="attend_back",
    )(q_t, keyed, valued, ctx_t, lse, d_a, d_b, extra)


def row_mean(value):
    return jnp.mean(value, axis=1, keepdims=True)


def normed(value):
    centred = value - row_mean(value)
    rate = lax.rsqrt(row_mean(centred * centred) + EPS)
    return centred * rate, rate


def norm_back(grad, hat, rate, gain):
    scaled = grad * gain
    return rate * (scaled - row_mean(scaled) - hat * row_mean(scaled * hat))


def column_sum(value):
    return jnp.sum(value, axis=0, keepdims=True)


def gelu(value):
    phi = 0.5 + 0.5 * lax.erf(value * (0.5**0.5))
    return phi, jnp.exp(value * value * -0.5) * (1.0 / math.sqrt(2.0 * math.pi))


def hidden_spans(hidden, chunk):
    return [(side, at, side * hidden + at) for side in range(2) for at in range(0, hidden, chunk)]


CHUNK = 512


def middle_kernel(count, parts, blocks, *rest):
    ctx_parts = rest[:parts]
    ctx_oth, x_ref, cot_ref, vectors, b_up = rest[parts : parts + 5]
    rest = rest[parts + 5 :]
    pieces = [rest[at : at + count] for at in range(0, 4 * count, count)]
    rest = rest[4 * count :]
    out, dz, dctx_own, dctx_oth, sums, sent_f, kept_f, sent_d, kept_d = rest[:9]
    w_own, w_oth, down_own, down_oth = rest[9:13]
    ctx_s, x_s, cot_s, act_s, slope_s, y_t, d_t, dz_t = rest[13:21]
    out_s, dz_s, dctx_s, tile, got_f, got_d, sems = rest[21:]
    wholes, downs = (w_own, w_oth), (down_own, down_oth)
    half = ctx_oth.shape[1]
    hidden = down_own.shape[1]
    width = x_ref.shape[1]
    mover = Mover(sems)
    stores = []

    inputs, at = [], 0
    for part in ctx_parts:
        size = part.shape[1]
        inputs.append(mover.start(part, ctx_s.at[0, :, pl.ds(at, size)]))
        at += size
    inputs.append(mover.start(ctx_oth, ctx_s.at[1]))
    loads = []
    for span in ((0, half), (half, hidden)):
        for side in range(2):
            loads.append(load_weight(mover, blocks, side, pieces[side], wholes[side], *span))
    for side in range(2):
        loads.append(load_weight(mover, blocks, side, pieces[2 + side], downs[side]))
    for place, load in enumerate(loads):
        for copy in load:
            copy.start()
        if place == 1:
            inputs.append(mover.start(x_ref, x_s))
    late = mover.start(cot_ref, cot_s)
    wait(inputs + loads[0] + loads[1])

    def put(tiles, lefts, rights, side, held, out_ref):
        for left, right, at, size, column in tiles:
            tile[:, :size] = dot(lefts[left][...], rights[right][:, at : at + size]).astype(BF16)
            store_pieces(blocks, [held], column, tile.at[:, pl.ds(0, size)], side)
            span = pl.ds(column, size)
            stores.append(mover.start(held.at[:, :, span], out_ref.at[:, :, span]))

    b_out, gain_one, shift_one = vectors[0:1, :], vectors[1:2, :], vectors[2:3, :]
    b_down, gain_two, shift_two = vectors[3:4, :], vectors[4:5, :], vectors[5:6, :]
    attn = dot(ctx_s[0], w_own[:, :half], 1, 1) + dot(ctx_s[1], w_oth[:, :half], 1, 1)
    hat_one, rate_one = normed(attn + b_out + x_s[...].astype(F32))
    y_one = hat_one * gain_one + shift_one
    low = y_one.astype(BF16)
    spans = hidden_spans(hidden, CHUNK)
    ffn = None
    wait(loads[2] + loads[3])

    def pre_of(side, at, _):
        pre = dot(low, wholes[side][:, half + at : half + at + CHUNK])
        return pre + b_up[side : side + 1, at : at + CHUNK]

    following = pre_of(*spans[0])
    for number, (side, at, place) in enumerate(spans):
        pre = following
        if number + 1 < len(spans):
            following = pre_of(*spans[number + 1])
        phi, bell = gelu(pre)
        act = (pre * phi).astype(BF16)
        act_s[:, place : place + CHUNK] = act
        slope_s[:, place : place + CHUNK] = (phi + pre * bell).astype(BF16)
        if number == 0:
            wait(loads[4] + loads[5])
        part = dot(act, downs[side][:, at : at + CHUNK], 1, 1)
        ffn = part if ffn is None else ffn + part
    hat_two, rate_two = normed(ffn + b_down + y_one)
    out_s[...] = (hat_two * gain_two + shift_two).astype(BF16)
    stores.append(mover.start(out_s, out))
    late.wait()
    cot = cot_s[...].astype(F32)
    d_two = norm_back(cot, hat_two, rate_two, gain_two)
    d_ffn = d_two.astype(BF16)
    d_t[...] = d_two.T.astype(BF16)
    y_t[...] = y_one.T.astype(BF16)
    sums[3:4, :] = column_sum(d_two)
    sums[4:5, :] = column_sum(cot * hat_two)
    sums[5:6, :] = column_sum(cot)
    for side, (held, out_ref) in ((1, (got_d.at[1], sent_d)), (0, (got_d.at[0], kept_d))):
        tiles = [(0, 0, side * hidden + at, CHUNK, at) for at in range(0, hidden, CHUNK)]
        put(tiles, [d_t], [act_s], side, held, out_ref)
    back = None

    def d_act_of(side, at, _):
        return dot(d_ffn, downs[side][:, at : at + CHUNK])

    following = d_act_of(*spans[0])
    for number, (side, at, place) in enumerate(spans):
        d_act = following
        if number + 1 < len(spans):
            following = d_act_of(*spans[number + 1])
        d_pre = (d_act * slope_s[:, place : place + CHUNK].astype(F32)).astype(BF16)
        slope_s[:, place : place + CHUNK] = d_pre
        total = column_sum(d_pre.astype(F32))
        for col in range(0, CHUNK, 256):
            spot = place + col
            row, left = 6 + spot // width, spot % width
            sums[row : row + 1, left : left + 256] = total[:, col : col + 256]
        part = dot(d_pre, wholes[side][:, half + at : half + at + CHUNK], 1, 1)
        back = part if back is None else back + part
    d_one = d_two + back
    d_zero = norm_back(d_one, hat_one, rate_one, gain_one)
    dz_s[...] = d_zero
    stores.append(mover.start(dz_s, dz))
    d_attn = d_zero.astype(BF16)
    dctx_s[0] = dot(d_attn, w_own[:, :half]).astype(BF16)
    dctx_s[1] = dot(d_attn, w_oth[:, :half]).astype(BF16)
    stores.append(mover.start(dctx_s.at[0], dctx_own))
    stores.append(mover.start(dctx_s.at[1], dctx_oth))
    dz_t[...] = d_zero.T.astype(BF16)
    sums[0:1, :] = column_sum(d_zero)
    sums[1:2, :] = column_sum(d_one * hat_one)
    sums[2:3, :] = column_sum(d_one)
    for side, (held, out_ref) in ((1, (got_f.at[1], sent_f)), (0, (got_f.at[0], kept_f))):
        tiles = [
            (1, 1, side * hidden + at, CHUNK, half + at) for at in range(0, hidden, CHUNK)
        ] + [(0, 0, 0, half, 0)]
        put(tiles, [dz_t, y_t], [ctx_s.at[side], slope_s], 2 + side, held, out_ref)
    wait(stores)


def middle(blocks, ctx_parts, ctx_oth, own, cotangent, vectors, b_up, pieces):
    rows, width = own.shape
    half = ctx_oth.shape[1]
    hidden = b_up.shape[1]
    shape = jax.ShapeDtypeStruct
    count = len(pieces[0])
    sum_rows = 6 + 2 * hidden // width
    flops = 2 * rows * width * (6 * half + 12 * hidden)
    number = blocks.shape[1]
    first = (number, width // number, half + hidden)
    down = (number, width // number, hidden)
    vmem = pltpu.VMEM
    return pl.pallas_call(
        functools.partial(middle_kernel, count, len(ctx_parts)),
        in_specs=[SCALARS]
        + [LEFT] * (len(ctx_parts) + 3)
        + [WHOLE, WHOLE]
        + [LEFT] * (4 * count),
        out_specs=[LEFT] * 4 + [WHOLE] + [LEFT] * 4,
        out_shape=[
            shape((rows, width), BF16),
            shape((rows, width), F32),
            shape((rows, half), BF16),
            shape((rows, half), BF16),
            shape((sum_rows, width), F32),
            shape(first, BF16),
            shape(first, BF16),
            shape(down, BF16),
            shape(down, BF16),
        ],
        scratch_shapes=[vmem((width, half + hidden), BF16)] * 2
        + [vmem((width, hidden), BF16)] * 2
        + [
            vmem((2, rows, half), BF16),
            vmem((rows, width), BF16),
            vmem((rows, width), BF16),
            vmem((rows, 2 * hidden), BF16),
            vmem((rows, 2 * hidden), BF16),
            vmem((width, rows), BF16),
            vmem((width, rows), BF16),
            vmem((width, rows), BF16),
            vmem((rows, width), BF16),
            vmem((rows, width), F32),
            vmem((2, rows, half), BF16),
            vmem((width, CHUNK), BF16),
            vmem((2, *first), BF16),
            vmem((2, *down), BF16),
            pltpu.SemaphoreType.DMA((144,)),
        ],
        compiler_params=params(),
        cost_estimate=cost(flops, 28 << 20, rows * hidden * 4),
        name="middle",
    )(
        blocks,
        *ctx_parts,
        ctx_oth,
        own,
        cotangent,
        vectors,
        b_up,
        *[piece for group in pieces for piece in group],
    )


def pair_places(parts):
    return [
        (group, at) for group, part in enumerate(parts) for at in range(0, part[0].shape[1], PAIR)
    ]


def grad_qkv_kernel(groups, blocks, x_t, *refs):
    parts = [refs[3 * group : 3 * group + 3] for group in range(groups)]
    refs = refs[3 * groups :]
    x_s, right_s, tile, sems = refs[-4:]
    outs, held = refs[:-6], refs[-6:-4]
    held = held[: len(outs)]
    mover = Mover(sems)
    loads = [mover.start(x_t, x_s)]
    places = pair_places(parts)
    for pair, (group, at) in enumerate(places):
        loads.append(
            [
                mover.start(
                    part.at[:, pl.ds(at, PAIR)], right_s.at[pair, :, pl.ds(kind * PAIR, PAIR)]
                )
                for kind, part in enumerate(parts[group])
            ]
        )
    loads[0].wait()
    stores = []
    for pair in range(len(places)):
        wait(loads[1 + pair])
        tile[...] = dot(x_s[...], right_s[pair]).astype(BF16)
        column = 3 * PAIR * pair
        store_pieces(blocks, held, column, tile)
        span = pl.ds(column, 3 * PAIR)
        for mine, out in zip(held, outs):
            stores.append(mover.start(mine.at[:, :, span], out.at[:, :, span]))
    wait(stores)


def grad_qkv_pieces(blocks, x_t, d_parts):
    width, seq = x_t.shape
    flat = [part for parts in d_parts for part in parts]
    columns = sum(part.shape[1] for part in flat)
    shapes = piece_shapes(blocks.shape[1], width, columns)
    held = [pltpu.VMEM(one.shape, BF16) for one in shapes]
    held += [pltpu.VMEM((8, 128), BF16)] * (2 - len(held))
    return pl.pallas_call(
        functools.partial(grad_qkv_kernel, len(d_parts)),
        in_specs=[SCALARS] + [LEFT] * (1 + len(flat)),
        out_specs=[LEFT] * len(shapes),
        out_shape=shapes,
        scratch_shapes=held
        + [
            pltpu.VMEM((width, seq), BF16),
            pltpu.VMEM((columns // (3 * PAIR), seq, 3 * PAIR), BF16),
            pltpu.VMEM((width, 3 * PAIR), BF16),
            pltpu.SemaphoreType.DMA((32,)),
        ],
        compiler_params=params(),
        cost_estimate=cost(2 * seq * width * columns, 6 << 20),
        name="grad_qkv",
    )(blocks, x_t, *flat)


def input_kernel(count, groups, blocks, *refs):
    parts = [refs[3 * group : 3 * group + 3] for group in range(groups)]
    refs = refs[3 * groups :]
    dz, pieces = refs[0], refs[1 : 1 + count]
    kept, sent, weight, whole, dz_s, sent_s, sems = refs[1 + count :]
    mover = Mover(sems)
    rows = kept.shape[0]
    half = whole.shape[1] // 3
    loads = load_weight(mover, blocks, 0, pieces, weight)
    for pair, (group, at) in enumerate(pair_places(parts)):
        for kind, part in enumerate(parts[group]):
            target = whole.at[:, pl.ds(kind * half + pair * PAIR, PAIR)]
            loads.append(mover.copy(part.at[:, pl.ds(at, PAIR)], target))
    for copy in loads:
        copy.start()
    last = mover.start(dz, dz_s)
    wait(loads)
    sent_s[...] = dot(whole[rows:, :], weight[...], 1, 1).astype(BF16)
    store = mover.start(sent_s, sent)
    last.wait()
    dz_s[...] += dot(whole[:rows, :], weight[...], 1, 1)
    mover.start(dz_s, kept).wait()
    store.wait()


def input_grad(blocks, d_parts, dz, pieces):
    rows, width = dz.shape
    flat = [part for parts in d_parts for part in parts]
    columns = sum(part.shape[1] for part in flat)
    shape = jax.ShapeDtypeStruct
    return pl.pallas_call(
        functools.partial(input_kernel, len(pieces), len(d_parts)),
        in_specs=[SCALARS] + [LEFT] * (len(flat) + 1 + len(pieces)),
        out_specs=[LEFT] * 2,
        out_shape=[shape((rows, width), F32), shape((rows, width), BF16)],
        scratch_shapes=[
            pltpu.VMEM((width, columns), BF16),
            pltpu.VMEM((2 * rows, columns), BF16),
            pltpu.VMEM((rows, width), F32),
            pltpu.VMEM((rows, width), BF16),
            pltpu.SemaphoreType.DMA((48,)),
        ],
        compiler_params=params(),
        cost_estimate=cost(4 * rows * width * columns, 8 << 20),
        name="input_grad",
    )(blocks, *flat, dz, *pieces)


def per_device(
    layer_in,
    seq_lens,
    w_qkv,
    b_qv,
    w_out,
    b_out,
    gain_one,
    shift_one,
    w_up,
    b_up,
    w_down,
    b_down,
    gain_two,
    shift_two,
    cotangent,
):
    rows, width = layer_in.shape
    seq = 2 * rows
    side = lax.axis_index("tensor")
    shard_rows, _, half = w_qkv.shape
    hidden = w_up.shape[1]
    blocks = row_blocks(side)
    pairs = range(half // PAIR)

    gather_qkv = Gather(w_qkv.reshape(shard_rows, 3 * half))
    gather_first = Gather(jnp.concatenate([w_out, w_up], axis=1))
    gather_down = Gather(w_down)
    oth_in = swap(layer_in)
    qkv_0 = gather_qkv.step()
    gather_first.step(qkv_0)
    qkv_1 = gather_qkv.step()
    gather_first.step(qkv_1)
    qkv_2 = gather_qkv.step()
    gather_down.step(qkv_2)
    qkv_3 = gather_qkv.step()
    gather_first.step(qkv_3)
    x_t = jnp.concatenate([after(layer_in, qkv_0), oth_in], axis=0).T

    bias_qv = lax.dynamic_slice_in_dim(b_qv, side * half, half, 1)
    bias = jnp.concatenate([bias_qv[0:1], jnp.zeros((1, half), F32), bias_qv[1:2]], axis=1)
    row = jnp.arange(seq, dtype=jnp.int32)
    position = ((row // rows) ^ side) * rows + row % rows
    lane = jnp.arange(PAIR, dtype=jnp.int32)[None, :]
    masked = jnp.where(position < seq_lens[0], 0.0, NEG)[:, None]
    extra = jnp.where(lane < 3, 1.0, jnp.where(lane == 3, masked, 0.0)).astype(BF16)

    q_t, keyed, valued = project(blocks, layer_in, oth_in, bias, gather_qkv.pieces)
    gather_down.step(qkv_3)
    gather_first.step()
    gather_down.step(q_t)
    first_pieces, down_pieces = gather_first.pieces, gather_down.pieces
    attended = [
        attend(0, 1, after(q_t, gather_first.sent), keyed, valued, extra)
    ]
    gather_down.step(attended[0][3])
    down_pieces = gather_down.pieces
    first_oth = [swap(after(first_pieces[0], attended[0][3]))]
    attended.append(
        attend(1, 2, after(q_t, attended[0][3], gather_down.sent), keyed, valued, extra)
    )
    first_oth += [swap(after(piece, attended[1][3])) for piece in first_pieces[1:]]
    down_oth = [swap(after(down_pieces[0], attended[1][3]))]
    attended.append(attend(2, 3, after(q_t, attended[1][3]), keyed, valued, extra))
    down_oth += [swap(after(piece, attended[2][3])) for piece in down_pieces[1:]]
    ctx_parts = [one[0] for one in attended]
    ctx_oth = swap(jnp.concatenate([one[1] for one in attended], axis=1))
    up_parts = b_up.reshape(2, hidden)
    up_bias = jnp.where(side == 0, up_parts, up_parts[::-1])
    vectors = jnp.stack([b_out, gain_one, shift_one, b_down, gain_two, shift_two])
    output, dz, dctx_own, dctx_oth, sums, sent_f, kept_f, sent_d, kept_d = middle(
        blocks,
        ctx_parts,
        ctx_oth,
        layer_in,
        cotangent,
        vectors,
        up_bias,
        [first_pieces, first_oth, down_pieces, down_oth],
    )
    d_ctx_b = swap(dctx_oth)
    scatter_down = Scatter([kept_d, swap(after(sent_d, d_ctx_b))], added=True)
    scatter_first = Scatter([kept_f, swap(after(sent_f, d_ctx_b))], 1, added=True)

    up_rows = hidden // width

    def back(group, first, last, *others):
        ctx_t, lse = attended[group][2:]
        return attend_back(
            first, last, after(q_t, *others), keyed, valued, ctx_t, lse, dctx_own, d_ctx_b, extra
        )

    backs = [back(0, 0, 1)]
    scatter_down.step(backs[0][3])
    first_3 = scatter_first.step(backs[0][3])
    backs.append(back(1, 1, 2, backs[0][3], scatter_down.sent, scatter_first.sent))
    down_2 = scatter_down.step(backs[1][3])
    backs.append(back(2, 2, 3, backs[1][3]))
    d_parts = [one[:3] for one in backs]
    qkv_kept = grad_qkv_pieces(blocks, x_t, d_parts)
    qv = jnp.concatenate([one[3][:2] for one in backs], axis=1).reshape(1, 2 * half)
    small = jnp.concatenate([sums, qv], axis=0)
    small = jnp.pad(small, ((0, 16 - small.shape[0]), (0, 0)))
    scatter_qkv = Scatter(qkv_kept, extra=small)
    scatter_qkv.step()
    scatter_down.step(qkv_kept[0])
    kept, sent = input_grad(
        blocks, d_parts, after(dz, qkv_kept[0], down_2), gather_qkv.pieces
    )
    first_2 = scatter_first.step(kept)
    oth_dx = swap(sent)
    qkv_2 = scatter_qkv.step(scatter_first.sent)
    scatter_first.step(kept)
    scatter_down.step(kept)
    grad_input = (kept + oth_dx.astype(F32)).astype(BF16)
    scatter_qkv.step(first_2)
    scatter_first.step(qkv_2)
    scatter_qkv.step()
    both = scatter_qkv.extra
    oth = swap(both)
    norms = both[:6] + oth[:6]
    grad_bup = both[6 : 6 + up_rows] + oth[6 + up_rows : 6 + 2 * up_rows]
    grad_bqv = both[6 + 2 * up_rows].reshape(2, half)
    grad_qkv = scatter_qkv.result().reshape(shard_rows, half // PAIR, 3, PAIR).transpose(0, 2, 1, 3)
    grad_first, grad_down = scatter_first.result(), scatter_down.result()

    return (
        output,
        grad_input,
        grad_qkv.reshape(shard_rows, 3, half),
        grad_bqv,
        grad_first[:, :half],
        norms[0],
        norms[1],
        norms[2],
        grad_first[:, half:],
        grad_bup.reshape(hidden),
        grad_down,
        norms[3],
        norms[4],
        norms[5],
    )


def solution(mesh):
    placed = (
        P(("dp", "tensor"), None),
        P("dp"),
        P("dp", None, "tensor"),
        P(),
        P("dp", "tensor"),
        P(),
        P(),
        P(),
        P("dp", "tensor"),
        P(),
        P("dp", "tensor"),
        P(),
        P(),
        P(),
        P(("dp", "tensor"), None),
    )
    return jax.shard_map(
        per_device,
        mesh=mesh,
        in_specs=placed,
        out_specs=(
            P(("dp", "tensor"), None),
            P(("dp", "tensor"), None),
            P("dp", None, "tensor"),
            P(None, "tensor"),
            P("dp", "tensor"),
            P(),
            P(),
            P(),
            P("dp", "tensor"),
            P("tensor"),
            P("dp", "tensor"),
            P(),
            P(),
            P(),
        ),
        check_vma=False,
    )
```
